512 devices in a mesh: ctx: 64 (over z, y_lo, core), kvh: 8 (over y_hi, x).
Axes of the slice: x: 4, y: 8 (y_hi: 2, y_lo: 4; y = y_hi * 4 + y_lo), z: 8, core: 2. Of those that a mesh axis runs over, the one named last changes fastest.
Arguments:
- query: bfloat16 [8192, 4096], P('ctx', 'kvh'), may hold values from -6 to 6, as said below
- key_rows: bfloat16 [8192, 1024], P('ctx', 'kvh'), may hold values from -6 to 6, as said below
- value_rows: bfloat16 [8192, 1024], P('ctx', 'kvh'), may hold values from -6 to 6
- output: bfloat16 [8192, 4096], P('ctx', 'kvh'), may hold values from -6 to 6
- grad_out: bfloat16 [8192, 4096], P('ctx', 'kvh'), may hold values from -6 to 6
- block_order: int32 [128], P('ctx'), may hold values from 0 to 127, as said below
- segment: int32 [8192], P('ctx'), may hold values from 0 to 4, as said below
Outputs:
- grad_query: bfloat16 [8192, 4096], P('ctx', 'kvh')
- grad_key: bfloat16 [8192, 1024], P('ctx', 'kvh')
- grad_value: bfloat16 [8192, 1024], P('ctx', 'kvh')
The draws below stay inside these ranges and needn't reach their ends.
Inputs may be any that keep to these rules, and one draw needn't show every extreme that they name: `query`: rows are of order one; some rows may be far larger. `key_rows`: rows are of order one; some rows may be far larger. A permutation: stored block r holds positions block_order[r] * 64 to block_order[r] * 64 + 63 in order. `segment`: taken in order of position, document numbers start at 0, never fall, rise by one at each new document and reach the maximum.
All inputs are finite; a program needn't handle non-finite values.
Results may differ from the reference program's by a relative error of at most 0.0075.
Values may be sent and summed in bfloat16 or wider, within the bound.
No kernel may reach another device: no remote copies, remote signals or barrier semaphores. Data moves between devices by JAX's collectives and lax.ppermute only.
A program may use at most 64 MiB of HBM per device.

```python
import jax
import jax.numpy as jnp
from jax import lax

HEADS = 32
KV_HEADS = 8
HD = 128
BLK = 64
NBLK = 128
TOKENS = 8192


def layout_draw(key):
    permuted = jax.random.permutation(jax.random.fold_in(key, 201), NBLK).astype(jnp.int32)
    start_rows = jax.random.permutation(jax.random.fold_in(key, 202), TOKENS - 1)[:4].astype(jnp.int32) + 1
    starts = jnp.zeros((TOKENS,), jnp.int32).at[start_rows].set(1)
    seg_pos = jnp.cumsum(starts).astype(jnp.int32)
    seg_store = seg_pos.reshape(NBLK, BLK)[permuted].reshape(-1)
    return (permuted, seg_store)


def draw_block_order(key, part):
    permuted, seg_store = layout_draw(key)
    return permuted


def draw_segment(key, part):
    permuted, seg_store = layout_draw(key)
    return seg_store


def draw_key_rows(key, part):
    key = jax.random.fold_in(key, 7)
    drawn = jnp.clip(jax.random.normal(key, (TOKENS, KV_HEADS * HD), jnp.float32), -4.0, 4.0)
    return drawn.astype(jnp.bfloat16)


def draw_query(key, part):
    key = jax.random.fold_in(key, 8)
    drawn = jnp.clip(jax.random.normal(key, (TOKENS, HEADS * HD), jnp.float32), -4.0, 4.0)
    return drawn.astype(jnp.bfloat16)


def levels(stream_key, shape, cuts, least, high):
    def one(dim, blocks):
        heights = jax.random.uniform(jax.random.fold_in(jax.random.fold_in(stream_key, 6), dim), (blocks,), jnp.float32, least / len(cuts), high / len(cuts))
        return jnp.repeat(jnp.exp(heights), shape[dim] // blocks).reshape((-1,) + (1,) * (len(shape) - dim - 1))

    loudness = one(*cuts[0])
    for cut in cuts[1:]:
        loudness = loudness * one(*cut)
    return loudness


def centred(rng, shape, deviation, reach, pieces=(), held_as=jnp.bfloat16):
    entries = jax.random.normal(rng, shape, jnp.float32) * deviation
    if len(pieces) > 0:
        entries = levels(rng, shape, pieces, -0.22, 0.18) * entries
    return jnp.clip(entries, min=-reach, max=reach).astype(held_as)


def setup_inputs(seed: int = 0) -> dict:
    streams_of = jax.random.split(jax.random.key(seed), 8)
    query = draw_query(jax.random.fold_in(streams_of[7], 71), 0)
    key_rows = draw_key_rows(jax.random.fold_in(streams_of[7], 71), 0)
    value_rows = centred(streams_of[2], (TOKENS, KV_HEADS * HD), 1.0, 6.0, ((0, 64), (1, 8)))
    output = centred(streams_of[3], (TOKENS, HEADS * HD), 1.0, 6.0, ((0, 64), (1, 8)))
    grad_out = centred(streams_of[4], (TOKENS, HEADS * HD), 1.0, 6.0, ((0, 64), (1, 8)))
    block_order = draw_block_order(jax.random.fold_in(streams_of[7], 71), 0)
    segment = draw_segment(jax.random.fold_in(streams_of[7], 71), 0)
    return dict(query=query, key_rows=key_rows, value_rows=value_rows, output=output, grad_out=grad_out, block_order=block_order, segment=segment)


def reference(query, key_rows, value_rows, output, grad_out, block_order, segment):
    score_scale = HD ** -0.5
    groups = HEADS // KV_HEADS
    positions = (block_order[:, None] * BLK + jnp.arange(BLK, dtype=jnp.int32)[None, :]).reshape(-1)
    allowed = (positions[None, :] <= positions[:, None]) & (segment[None, :] == segment[:, None])

    def one_head(head_index):
        group_index = head_index // groups
        query_head = lax.dynamic_slice_in_dim(query, head_index * HD, HD, 1)
        grad_head = lax.dynamic_slice_in_dim(grad_out, head_index * HD, HD, 1)
        saved_head = lax.dynamic_slice_in_dim(output, head_index * HD, HD, 1)
        key_head = lax.dynamic_slice_in_dim(key_rows, group_index * HD, HD, 1)
        value_head = lax.dynamic_slice_in_dim(value_rows, group_index * HD, HD, 1)
        scores = jnp.dot(query_head, key_head.T, preferred_element_type=jnp.float32) * score_scale
        row_peak = jnp.max(jnp.where(allowed, scores, -jnp.inf), axis=1, keepdims=True)
        row_total = jnp.sum(jnp.where(allowed, jnp.exp(scores - row_peak), 0.0), axis=1, keepdims=True)
        log_total = row_peak + jnp.log(row_total)
        probs = jnp.where(allowed, jnp.exp(scores - log_total), 0.0)
        row_delta = jnp.sum(grad_head.astype(jnp.float32) * saved_head.astype(jnp.float32), axis=1, keepdims=True)
        dprobs = jnp.dot(grad_head, value_head.T, preferred_element_type=jnp.float32)
        dscores = probs * (dprobs - row_delta)
        probs_b = probs.astype(jnp.bfloat16)
        dscores_b = dscores.astype(jnp.bfloat16)
        d_query = jnp.dot(dscores_b, key_head, preferred_element_type=jnp.float32) * score_scale
        d_key = jnp.dot(dscores_b.T, query_head, preferred_element_type=jnp.float32) * score_scale
        d_value = jnp.dot(probs_b.T, grad_head, preferred_element_type=jnp.float32)
        return d_query, d_key, d_value

    all_query, all_key, all_value = lax.map(one_head, jnp.arange(HEADS, dtype=jnp.int32))
    tokens_all = query.shape[0]
    grad_query = all_query.transpose(1, 0, 2).reshape(tokens_all, HEADS * HD).astype(jnp.bfloat16)
    grad_key = all_key.reshape(KV_HEADS, groups, tokens_all, HD).sum(axis=1)
    grad_key = grad_key.transpose(1, 0, 2).reshape(tokens_all, KV_HEADS * HD).astype(jnp.bfloat16)
    grad_value = all_value.reshape(KV_HEADS, groups, tokens_all, HD).sum(axis=1)
    grad_value = grad_value.transpose(1, 0, 2).reshape(tokens_all, KV_HEADS * HD).astype(jnp.bfloat16)
    return grad_query, grad_key, grad_value
```

```python
import functools

import jax
import jax.numpy as jnp
from jax import lax
from jax.experimental import pallas as pl
from jax.experimental.pallas import tpu as pltpu
from jax.sharding import PartitionSpec as P

HEADS = 32
KV_HEADS = 8
HD = 128
GROUP = HEADS // KV_HEADS
BLK = 64
TOKENS = 8192
TOK = 128
EXTRA = 16
PAY = TOK + EXTRA
YS = 4
ZS = 8
QT = YS * TOK
KT = 2 * TOK
SCALE = HD**-0.5
EXP2 = SCALE * 1.4426950408889634
MASKED = -1e30
FLOOR = -1e25
F32 = jnp.float32
BF16 = jnp.bfloat16
VMEM_LIMIT = 24 * 1024 * 1024

NT = (((1,), (1,)), ((), ()))
TN = (((0,), (0,)), ((), ()))


def dot(a, b, dims=(((1,), (0,)), ((), ()))):
    return lax.dot_general(a, b, dims, preferred_element_type=F32)


def pack_kernel(order_ref, seg_ref, q_ref, k_ref, v_ref, o_ref, g_ref, qp_ref, kvp_ref):
    lane = lax.broadcasted_iota(jnp.int32, (1, TOK), 1)
    block = jnp.where(lane < BLK, order_ref[0], order_ref[1]).astype(F32)
    doc = seg_ref[...].astype(F32)
    qp_ref[0:TOK, 0 : GROUP * HD] = q_ref[...]
    qp_ref[0:TOK, GROUP * HD : 2 * GROUP * HD] = g_ref[...]
    highs, lows = [], []
    for h in range(GROUP):
        cols = slice(h * HD, (h + 1) * HD)
        prod = g_ref[:, cols].astype(F32) * o_ref[:, cols].astype(F32)
        delta = jnp.sum(prod.T, axis=0, keepdims=True)
        high = delta.astype(BF16).astype(F32)
        highs.append(high)
        lows.append(delta - high)
    first = jnp.concatenate(highs + lows, axis=1)
    zero = jnp.zeros_like(doc)
    second = jnp.concatenate([doc, block] + [zero] * 6, axis=1)
    row = lax.broadcasted_iota(jnp.int32, (EXTRA, 8 * TOK), 0)
    extra = jnp.where(row == 0, first, jnp.where(row == 1, second, 0.0))
    qp_ref[TOK:PAY, :] = extra.astype(BF16)
    kv_extra = jnp.concatenate([doc, block], axis=1)
    kv_extra = jnp.broadcast_to(kv_extra, (EXTRA, 2 * HD)).astype(BF16)
    for z in range(ZS):
        kvp_ref[z, 0:TOK, 0:HD] = k_ref[...]
        kvp_ref[z, 0:TOK, HD : 2 * HD] = v_ref[...]
        kvp_ref[z, TOK:PAY, :] = kv_extra


def code_of(doc, block):
    lane = lax.broadcasted_iota(jnp.int32, doc.shape, 1)
    within = jnp.where(lane < BLK, lane, lane - BLK).astype(F32)
    return doc * TOKENS + block * BLK + within


def score_kernel(n_prev, *refs):
    kv_ref, *rest = refs
    q_refs, rest = rest[:YS], rest[YS:]
    if n_prev:
        y_ref, prev_ref, pt_ref, st_ref, fin_ref, qs, code, bias, keep = rest
    else:
        pt_ref, st_ref, qs, code, bias = rest
    step = pl.program_id(0)

    @pl.when(step == 0)
    def _():
        for x, q_ref in enumerate(q_refs):
            toks = slice(x * TOK, (x + 1) * TOK)
            for h in range(GROUP):
                qs[h, toks, :] = q_ref[0:TOK, h * HD : (h + 1) * HD]
            info = q_ref[TOK:PAY, :].astype(F32)
            doc, block = info[1:2, 0:TOK], info[1:2, TOK : 2 * TOK]
            code[0:1, toks] = code_of(doc, block)
            code[1:2, toks] = doc * TOKENS

    for b in range(2):
        info = kv_ref[b, TOK:PAY, :].astype(F32)
        key_code = code_of(info[0:1, 0:TOK], info[0:1, TOK : 2 * TOK])
        key_code = jnp.broadcast_to(key_code, (TOK, TOK)).T
        for x in range(YS):
            toks = slice(x * TOK, (x + 1) * TOK)
            ok = (key_code <= code[0:1, toks]) & (key_code >= code[1:2, toks])
            bias[b * TOK : (b + 1) * TOK, toks] = jnp.where(ok, 0.0, MASKED)
    keys = jnp.concatenate([kv_ref[0, 0:TOK, 0:HD], kv_ref[1, 0:TOK, 0:HD]], axis=0)
    for h in range(GROUP):
        s = dot(keys, qs[h], NT) + bias[...]
        peak = jnp.maximum(jnp.max(s, axis=0, keepdims=True), FLOOR)
        p = jnp.exp2((s - peak) * EXP2)
        st_ref[0, h : h + 1, :] = peak
        st_ref[0, GROUP + h : GROUP + h + 1, :] = jnp.sum(p, axis=0, keepdims=True)
        pt_ref[:, h * QT : (h + 1) * QT] = p.astype(BF16)
    if n_prev:
        keep[pl.ds(step, 1)] = st_ref[...]

        @pl.when(step == pl.num_programs(0) - 1)
        def _():
            tiles = [prev_ref[t] for t in range(n_prev)] + [keep[t] for t in range(n_prev)]
            top = functools.reduce(jnp.maximum, [t[0:GROUP] for t in tiles])
            total = sum(t[GROUP:] * jnp.exp2((t[0:GROUP] - top) * EXP2) for t in tiles)
            for d in range(YS):
                for x in range(YS):
                    to, of = slice(x * TOK, (x + 1) * TOK), slice((x ^ d) * TOK, ((x ^ d) + 1) * TOK)
                    fin_ref[y_ref[0] ^ d, 0:GROUP, to] = top[:, of]
                    fin_ref[y_ref[0] ^ d, GROUP : 2 * GROUP, to] = total[:, of]


def grad_kernel(last, kv_ref, pt_ref, st_ref, all_ref, q0, q1, q2, q3, *rest):
    if last:
        dq_in, dkv_ref, own_ref, send1, send2, send3, qs, gs, delta, dq = rest
    else:
        dkv_ref, dq, qs, gs, delta = rest
    step = pl.program_id(0)

    @pl.when(step == 0)
    def _():
        for x, q_ref in enumerate((q0, q1, q2, q3)):
            toks = slice(x * TOK, (x + 1) * TOK)
            for h in range(GROUP):
                qs[h, toks, :] = q_ref[0:TOK, h * HD : (h + 1) * HD]
                gs[h, toks, :] = q_ref[0:TOK, (GROUP + h) * HD : (GROUP + h + 1) * HD]
            info = q_ref[TOK:PAY, :].astype(F32)
            for h in range(GROUP):
                high = info[0:1, h * TOK : (h + 1) * TOK]
                low = info[0:1, (GROUP + h) * TOK : (GROUP + h + 1) * TOK]
                delta[h : h + 1, toks] = high + low
        dq[...] = dq_in[...] if last else jnp.zeros_like(dq)

    top = functools.reduce(jnp.maximum, [all_ref[y, 0:GROUP] for y in range(YS)])
    total = sum(
        all_ref[y, GROUP : 2 * GROUP] * jnp.exp2((all_ref[y, 0:GROUP] - top) * EXP2)
        for y in range(YS)
    )
    weight = jnp.exp2((st_ref[0, 0:GROUP] - top) * EXP2) / total
    keys = jnp.concatenate([kv_ref[0, 0:TOK, 0:HD], kv_ref[1, 0:TOK, 0:HD]], axis=0)
    values = jnp.concatenate(
        [kv_ref[0, 0:TOK, HD : 2 * HD], kv_ref[1, 0:TOK, HD : 2 * HD]], axis=0
    )
    dk = jnp.zeros((KT, HD), F32)
    dv = jnp.zeros((KT, HD), F32)
    for h in range(GROUP):
        dp = dot(values, gs[h], NT)
        p = pt_ref[:, h * QT : (h + 1) * QT].astype(F32) * weight[h : h + 1]
        ds = (p * (dp - delta[h : h + 1, :])).astype(BF16)
        dv = dv + dot(p.astype(BF16), gs[h])
        dk = dk + dot(ds, qs[h])
        dq[h] += dot(keys, ds, TN)
    dk = dk * SCALE
    for b in range(2):
        rows = slice(b * TOK, (b + 1) * TOK)
        dkv_ref[b, :, 0:HD] = dk[rows].astype(dkv_ref.dtype)
        dkv_ref[b, :, HD : 2 * HD] = dv[rows].astype(dkv_ref.dtype)

    if last:

        @pl.when(step == pl.num_programs(0) - 1)
        def _():
            for x, out in enumerate((own_ref, send1, send2, send3)):
                for h in range(GROUP):
                    part = dq[h, :, x * TOK : (x + 1) * TOK].T * SCALE
                    out[:, h * HD : (h + 1) * HD] = part.astype(out.dtype)


def whole(shape):
    return pl.BlockSpec(shape, lambda *_: (0,) * len(shape))


def shape_of(shape, dtype):
    return jax.ShapeDtypeStruct(shape, dtype)


def params():
    return pltpu.CompilerParams(vmem_limit_bytes=VMEM_LIMIT)


def pack(order, seg, q, k, v, o, g):
    vm = pl.BlockSpec(memory_space=pltpu.VMEM)
    return pl.pallas_call(
        pack_kernel,
        out_shape=(shape_of((PAY, 2 * GROUP * HD), BF16), shape_of((ZS, PAY, 2 * HD), BF16)),
        in_specs=[pl.BlockSpec(memory_space=pltpu.SMEM)] + [vm] * 6,
        out_specs=(vm, vm),
        compiler_params=params(),
        name="pack",
    )(order, seg, q, k, v, o, g)


STEPS = ZS // 2
PAIRS = ZS * TOK * GROUP * QT


def scores(kv, queries, prev=None, y_index=None):
    in_specs = [pl.BlockSpec((2, PAY, 2 * HD), lambda i: (i, 0, 0))]
    in_specs += [whole((PAY, 2 * GROUP * HD))] * YS
    args = [kv, *queries]
    out_shape = [
        shape_of((ZS * TOK, GROUP * QT), BF16),
        shape_of((STEPS, 2 * GROUP, QT), F32),
    ]
    out_specs = [
        pl.BlockSpec((KT, GROUP * QT), lambda i: (i, 0)),
        pl.BlockSpec((1, 2 * GROUP, QT), lambda i: (i, 0, 0)),
    ]
    scratch = [
        pltpu.VMEM((GROUP, QT, HD), BF16),
        pltpu.VMEM((8, QT), F32),
        pltpu.VMEM((KT, QT), F32),
    ]
    if prev is not None:
        in_specs += [pl.BlockSpec(memory_space=pltpu.SMEM), whole(prev.shape)]
        args += [y_index, prev]
        out_shape.append(shape_of((YS, 2 * GROUP, QT), F32))
        out_specs.append(whole((YS, 2 * GROUP, QT)))
        scratch.append(pltpu.VMEM((STEPS, 2 * GROUP, QT), F32))
    return pl.pallas_call(
        functools.partial(score_kernel, 0 if prev is None else STEPS),
        grid=(STEPS,),
        in_specs=in_specs,
        out_specs=out_specs,
        out_shape=out_shape,
        scratch_shapes=scratch,
        compiler_params=params(),
        cost_estimate=pl.CostEstimate(
            flops=4 * PAIRS * HD, bytes_accessed=4 << 20, transcendentals=PAIRS
        ),
        name="scores",
    )(*args)


def grads(kv, probs, stats, all_stats, queries, dq_in=None):
    last = dq_in is not None
    in_specs = [
        pl.BlockSpec((2, PAY, 2 * HD), lambda i: (i, 0, 0)),
        pl.BlockSpec((KT, GROUP * QT), lambda i: (i, 0)),
        pl.BlockSpec((1, 2 * GROUP, QT), lambda i: (i, 0, 0)),
        whole((YS, 2 * GROUP, QT)),
    ] + [whole((PAY, 2 * GROUP * HD))] * YS
    args = [kv, probs, stats, all_stats, *queries]
    dkv_type = F32 if last else BF16
    out_shape = [shape_of((ZS, TOK, 2 * HD), dkv_type)]
    out_specs = [pl.BlockSpec((2, TOK, 2 * HD), lambda i: (i, 0, 0))]
    dq_shape = (GROUP, HD, QT)
    scratch = [
        pltpu.VMEM((GROUP, QT, HD), BF16),
        pltpu.VMEM((GROUP, QT, HD), BF16),
        pltpu.VMEM((8, QT), F32),
    ]
    if last:
        in_specs.append(whole(dq_shape))
        args.append(dq_in)
        out_shape += [shape_of((TOK, GROUP * HD), F32)]
        out_shape += [shape_of((TOK, GROUP * HD), BF16)] * (YS - 1)
        out_specs += [whole((TOK, GROUP * HD))] * YS
        scratch.append(pltpu.VMEM(dq_shape, F32))
    else:
        out_shape.append(shape_of(dq_shape, F32))
        out_specs.append(whole(dq_shape))
    return pl.pallas_call(
        functools.partial(grad_kernel, last),
        grid=(STEPS,),
        in_specs=in_specs,
        out_specs=out_specs,
        out_shape=out_shape,
        scratch_shapes=scratch,
        compiler_params=params(),
        cost_estimate=pl.CostEstimate(
            flops=16 * PAIRS * HD, bytes_accessed=4 << 20, transcendentals=0
        ),
        name="grads",
    )(*args)


def per_device(query, key_rows, value_rows, output, grad_out, block_order, segment):
    n = lax.axis_size("ctx")
    z_groups = [[z * 2 * YS + r for z in range(ZS)] for r in range(2 * YS)]
    y_groups = [
        [z * 2 * YS + y * 2 + c for y in range(YS)] for z in range(ZS) for c in range(2)
    ]

    def swap(x, bits):
        return lax.ppermute(x, "ctx", [(i, i ^ bits) for i in range(n)])

    def exchange(x, groups):
        return lax.all_to_all(x, "ctx", 0, 0, tiled=True, axis_index_groups=groups)

    q_pay, kv_pay = pack(
        block_order, segment.reshape(1, TOK), query, key_rows, value_rows, output, grad_out
    )
    kv_own = exchange(kv_pay, z_groups)
    queries = [q_pay] + [swap(q_pay, 2 * x) for x in range(1, YS)]
    kv_twin = swap(kv_own, 1)
    p_own, st_own = scores(kv_own, queries)
    y_index = (lax.axis_index("ctx") // 2 % YS).astype(jnp.int32).reshape(1)
    p_twin, st_twin, stats = scores(kv_twin, queries, st_own, y_index)
    all_stats = exchange(stats, y_groups)
    dkv_twin, dq = grads(kv_twin, p_twin, st_twin, all_stats, queries)
    dkv_back = swap(dkv_twin, 1)
    dkv_own, dq_own, *dq_send = grads(kv_own, p_own, st_own, all_stats, queries, dq)
    dkv = (dkv_own + dkv_back.astype(F32)).astype(BF16)
    dkv_all = exchange(dkv, z_groups)
    dq_parts = [swap(part, 2 * x) for x, part in enumerate(dq_send, 1)]
    grad_query = dq_own + sum(part.astype(F32) for part in dq_parts)
    grad_kv = jnp.sum(dkv_all.astype(F32), axis=0).astype(BF16)
    return grad_query.astype(BF16), grad_kv[:, 0:HD], grad_kv[:, HD : 2 * HD]


def solution(mesh):
    both = P("ctx", "kvh")
    return jax.shard_map(
        per_device,
        mesh=mesh,
        in_specs=(both, both, both, both, both, P("ctx"), P("ctx")),
        out_specs=(both, both, both),
        check_vma=False,
    )
```

```python
import functools

import jax
import jax.numpy as jnp
from jax import lax
from jax.experimental import pallas as pl
from jax.experimental.pallas import tpu as pltpu
from jax.sharding import PartitionSpec as P

HEADS = 32
KV_HEADS = 8
HD = 128
GROUP = HEADS // KV_HEADS
BLK = 64
TOKENS = 8192
TOK = 128
EXTRA = 16
PAY = TOK + EXTRA
YS = 4
ZS = 8
QT = YS * TOK
KT = 2 * TOK
SCALE = HD**-0.5
EXP2 = SCALE * 1.4426950408889634
MASKED = -1e30
FLOOR = -1e25
F32 = jnp.float32
BF16 = jnp.bfloat16
VMEM_LIMIT = 57

NT = (((1,), (1,)), ((), ()))
TN = (((0,), (0,)), ((), ()))


def dot(a, b, dims=(((1,), (0,)), ((), ()))):
    return lax.dot_general(a, b, dims, preferred_element_type=F32)


def pack_kernel(
    order_hbm, seg_hbm, q_hbm, k_hbm, v_hbm, o_hbm, g_hbm, kvp_hbm, qp_ref, gp_ref,
    order_ref, seg_ref, kv_ref, o_ref, in_sems, out_sems,
):
    moves = (
        (order_hbm, order_ref),
        (seg_hbm, seg_ref),
        (k_hbm, kv_ref.at[0:TOK, 0:HD]),
        (v_hbm, kv_ref.at[0:TOK, HD : 2 * HD]),
        (q_hbm, qp_ref.at[0:TOK]),
        (g_hbm, gp_ref.at[0:TOK]),
        (o_hbm, o_ref),
    )
    copies = [
        pltpu.make_async_copy(src, dst, in_sems.at[i]) for i, (src, dst) in enumerate(moves)
    ]
    for copy in copies:
        copy.start()
    for copy in copies[:4]:
        copy.wait()
    lane = lax.broadcasted_iota(jnp.int32, (1, TOK), 1)
    block = jnp.where(lane < BLK, order_ref[0], order_ref[1]).astype(F32)
    doc = seg_ref[...].astype(F32)
    kv_extra = jnp.concatenate([doc, block], axis=1)
    kv_ref[TOK:PAY, :] = jnp.broadcast_to(kv_extra, (EXTRA, 2 * HD)).astype(BF16)
    outs = [
        pltpu.make_async_copy(kv_ref, kvp_hbm.at[z], out_sems.at[z]) for z in range(ZS)
    ]
    for copy in outs:
        copy.start()
    for copy in copies[4:]:
        copy.wait()
    highs, lows = [], []
    for h in range(GROUP):
        cols = slice(h * HD, (h + 1) * HD)
        prod = gp_ref[0:TOK, cols].astype(F32) * o_ref[:, cols].astype(F32)
        delta = jnp.sum(prod.T, axis=0, keepdims=True)
        high = delta.astype(BF16).astype(F32)
        highs.append(high)
        lows.append(delta - high)
    zero = jnp.zeros_like(doc)
    q_extra = jnp.concatenate([doc, block, zero, zero], axis=1)
    qp_ref[TOK:PAY, :] = jnp.broadcast_to(q_extra, (EXTRA, GROUP * HD)).astype(BF16)
    row = lax.broadcasted_iota(jnp.int32, (EXTRA, GROUP * HD), 0)
    g_extra = jnp.where(
        row == 0, jnp.concatenate(highs, axis=1), jnp.concatenate(lows, axis=1)
    )
    gp_ref[TOK:PAY, :] = g_extra.astype(BF16)
    for copy in outs:
        copy.wait()


def code_of(doc, block):
    lane = lax.broadcasted_iota(jnp.int32, doc.shape, 1)
    within = jnp.where(lane < BLK, lane, lane - BLK).astype(F32)
    return doc * TOKENS + block * BLK + within


def score_kernel(n_prev, *refs):
    kv_ref, *rest = refs
    q_refs, rest = rest[:YS], rest[YS:]
    if n_prev:
        y_ref, prev_ref, pt_ref, st_ref, fin_ref, qs, code, bias, keep = rest
    else:
        pt_ref, st_ref, qs, code, bias = rest
    step = pl.program_id(0)

    @pl.when(step == 0)
    def _():
        for x, q_ref in enumerate(q_refs):
            toks = slice(x * TOK, (x + 1) * TOK)
            for h in range(GROUP):
                qs[h, toks, :] = q_ref[0:TOK, h * HD : (h + 1) * HD]
            info = q_ref[TOK:PAY, :].astype(F32)
            doc, block = info[0:1, 0:TOK], info[0:1, TOK : 2 * TOK]
            code[0:1, toks] = code_of(doc, block)
            code[1:2, toks] = doc * TOKENS

    for b in range(2):
        info = kv_ref[b, TOK:PAY, :].astype(F32)
        key_code = code_of(info[0:1, 0:TOK], info[0:1, TOK : 2 * TOK])
        key_code = jnp.broadcast_to(key_code, (TOK, TOK)).T
        for x in range(YS):
            toks = slice(x * TOK, (x + 1) * TOK)
            ok = (key_code <= code[0:1, toks]) & (key_code >= code[1:2, toks])
            bias[b * TOK : (b + 1) * TOK, toks] = jnp.where(ok, 0.0, MASKED)
    keys = jnp.concatenate([kv_ref[0, 0:TOK, 0:HD], kv_ref[1, 0:TOK, 0:HD]], axis=0)
    for h in range(GROUP):
        s = dot(keys, qs[h], NT) + bias[...]
        peak = jnp.maximum(jnp.max(s, axis=0, keepdims=True), FLOOR)
        p = jnp.exp2((s - peak) * EXP2)
        st_ref[0, h : h + 1, :] = peak
        st_ref[0, GROUP + h : GROUP + h + 1, :] = jnp.sum(p, axis=0, keepdims=True)
        pt_ref[:, h * QT : (h + 1) * QT] = p.astype(BF16)
    if n_prev:
        keep[pl.ds(step, 1)] = st_ref[...]

        @pl.when(step == pl.num_programs(0) - 1)
        def _():
            tiles = [prev_ref[t] for t in range(n_prev)] + [keep[t] for t in range(n_prev)]
            top = functools.reduce(jnp.maximum, [t[0:GROUP] for t in tiles])
            total = sum(t[GROUP:] * jnp.exp2((t[0:GROUP] - top) * EXP2) for t in tiles)
            for d in range(YS):
                for x in range(YS):
                    to, of = slice(x * TOK, (x + 1) * TOK), slice((x ^ d) * TOK, ((x ^ d) + 1) * TOK)
                    fin_ref[y_ref[0] ^ d, 0:GROUP, to] = top[:, of]
                    fin_ref[y_ref[0] ^ d, GROUP : 2 * GROUP, to] = total[:, of]


def grad_kernel(last, kv_ref, pt_ref, st_ref, all_ref, *rest):
    q_refs, g_refs, rest = rest[:YS], rest[YS : 2 * YS], rest[2 * YS :]
    if last:
        dq_in, dkv_ref, own_ref, send1, send2, send3, qs, gs, delta, dq = rest
    else:
        dkv_ref, dq, qs, gs, delta = rest
    step = pl.program_id(0)

    @pl.when(step == 0)
    def _():
        for x, (q_ref, g_ref) in enumerate(zip(q_refs, g_refs)):
            toks = slice(x * TOK, (x + 1) * TOK)
            info = g_ref[TOK:PAY, :].astype(F32)
            for h in range(GROUP):
                cols = slice(h * HD, (h + 1) * HD)
                qs[h, toks, :] = q_ref[0:TOK, cols]
                gs[h, toks, :] = g_ref[0:TOK, cols]
                delta[h : h + 1, toks] = info[0:1, cols] + info[1:2, cols]
        dq[...] = dq_in[...] if last else jnp.zeros_like(dq)

    top = functools.reduce(jnp.maximum, [all_ref[y, 0:GROUP] for y in range(YS)])
    total = sum(
        all_ref[y, GROUP : 2 * GROUP] * jnp.exp2((all_ref[y, 0:GROUP] - top) * EXP2)
        for y in range(YS)
    )
    weight = jnp.exp2((st_ref[0, 0:GROUP] - top) * EXP2) / total
    keys = jnp.concatenate([kv_ref[0, 0:TOK, 0:HD], kv_ref[1, 0:TOK, 0:HD]], axis=0)
    values = jnp.concatenate(
        [kv_ref[0, 0:TOK, HD : 2 * HD], kv_ref[1, 0:TOK, HD : 2 * HD]], axis=0
    )
    dk = jnp.zeros((KT, HD), F32)
    dv = jnp.zeros((KT, HD), F32)
    for h in range(GROUP):
        dp = dot(values, gs[h], NT)
        p = pt_ref[:, h * QT : (h + 1) * QT].astype(F32) * weight[h : h + 1]
        ds = (p * (dp - delta[h : h + 1, :])).astype(BF16)
        dv = dv + dot(p.astype(BF16), gs[h])
        dk = dk + dot(ds, qs[h])
        dq[h] += dot(keys, ds, TN)
    dk = dk * SCALE
    for b in range(2):
        rows = slice(b * TOK, (b + 1) * TOK)
        dkv_ref[b, :, 0:HD] = dk[rows].astype(dkv_ref.dtype)
        dkv_ref[b, :, HD : 2 * HD] = dv[rows].astype(dkv_ref.dtype)

    if last:

        @pl.when(step == pl.num_programs(0) - 1)
        def _():
            for x, out in enumerate((own_ref, send1, send2, send3)):
                for h in range(GROUP):
                    part = dq[h, :, x * TOK : (x + 1) * TOK].T * SCALE
                    out[:, h * HD : (h + 1) * HD] = part.astype(out.dtype)


def whole(shape):
    return pl.BlockSpec(shape, lambda *_: (0,) * len(shape))


def shape_of(shape, dtype):
    return jax.ShapeDtypeStruct(shape, dtype)


def params(limit=VMEM_LIMIT):
    return pltpu.CompilerParams(vmem_limit_bytes=limit << 20)


def pack(order, seg, q, k, v, o, g):
    hbm = pl.BlockSpec(memory_space=pltpu.HBM)
    vm = pl.BlockSpec(memory_space=pltpu.VMEM)
    pay = shape_of((PAY, GROUP * HD), BF16)
    return pl.pallas_call(
        pack_kernel,
        out_shape=(shape_of((ZS, PAY, 2 * HD), BF16), pay, pay),
        in_specs=[hbm] * 7,
        out_specs=(hbm, vm, vm),
        scratch_shapes=[
            pltpu.SMEM((2,), jnp.int32),
            pltpu.VMEM((1, TOK), jnp.int32),
            pltpu.VMEM((PAY, 2 * HD), BF16),
            pltpu.VMEM((TOK, GROUP * HD), BF16),
            pltpu.SemaphoreType.DMA((7,)),
            pltpu.SemaphoreType.DMA((ZS,)),
        ],
        compiler_params=params(60),
        name="pack",
    )(order, seg, q, k, v, o, g)


STEPS = ZS // 2
PAIRS = ZS * TOK * GROUP * QT


def scores(kv, queries, prev=None, y_index=None):
    in_specs = [pl.BlockSpec((2, PAY, 2 * HD), lambda i: (i, 0, 0))]
    in_specs += [whole((PAY, GROUP * HD))] * YS
    args = [kv, *queries]
    out_shape = [
        shape_of((ZS * TOK, GROUP * QT), BF16),
        shape_of((STEPS, 2 * GROUP, QT), F32),
    ]
    out_specs = [
        pl.BlockSpec((KT, GROUP * QT), lambda i: (i, 0)),
        pl.BlockSpec((1, 2 * GROUP, QT), lambda i: (i, 0, 0)),
    ]
    scratch = [
        pltpu.VMEM((GROUP, QT, HD), BF16),
        pltpu.VMEM((8, QT), F32),
        pltpu.VMEM((KT, QT), F32),
    ]
    if prev is not None:
        in_specs += [pl.BlockSpec(memory_space=pltpu.SMEM), whole(prev.shape)]
        args += [y_index, prev]
        out_shape.append(shape_of((YS, 2 * GROUP, QT), F32))
        out_specs.append(whole((YS, 2 * GROUP, QT)))
        scratch.append(pltpu.VMEM((STEPS, 2 * GROUP, QT), F32))
    return pl.pallas_call(
        functools.partial(score_kernel, 0 if prev is None else STEPS),
        grid=(STEPS,),
        in_specs=in_specs,
        out_specs=out_specs,
        out_shape=out_shape,
        scratch_shapes=scratch,
        compiler_params=params(),
        cost_estimate=pl.CostEstimate(
            flops=PAIRS, bytes_accessed=1 << 16, transcendentals=0
        ),
        name="scores",
    )(*args)


def grads(kv, probs, stats, all_stats, queries, outs, dq_in=None):
    last = dq_in is not None
    in_specs = [
        pl.BlockSpec((2, PAY, 2 * HD), lambda i: (i, 0, 0)),
        pl.BlockSpec((KT, GROUP * QT), lambda i: (i, 0)),
        pl.BlockSpec((1, 2 * GROUP, QT), lambda i: (i, 0, 0)),
        whole((YS, 2 * GROUP, QT)),
    ] + [whole((PAY, GROUP * HD))] * (2 * YS)
    args = [kv, probs, stats, all_stats, *queries, *outs]
    dkv_type = F32 if last else BF16
    out_shape = [shape_of((ZS, TOK, 2 * HD), dkv_type)]
    out_specs = [pl.BlockSpec((2, TOK, 2 * HD), lambda i: (i, 0, 0))]
    dq_shape = (GROUP, HD, QT)
    scratch = [
        pltpu.VMEM((GROUP, QT, HD), BF16),
        pltpu.VMEM((GROUP, QT, HD), BF16),
        pltpu.VMEM((8, QT), F32),
    ]
    if last:
        in_specs.append(whole(dq_shape))
        args.append(dq_in)
        out_shape += [shape_of((TOK, GROUP * HD), F32)]
        out_shape += [shape_of((TOK, GROUP * HD), BF16)] * (YS - 1)
        out_specs += [whole((TOK, GROUP * HD))] * YS
        scratch.append(pltpu.VMEM(dq_shape, F32))
    else:
        out_shape.append(shape_of(dq_shape, F32))
        out_specs.append(whole(dq_shape))
    return pl.pallas_call(
        functools.partial(grad_kernel, last),
        grid=(STEPS,),
        in_specs=in_specs,
        out_specs=out_specs,
        out_shape=out_shape,
        scratch_shapes=scratch,
        compiler_params=params(),
        cost_estimate=pl.CostEstimate(
            flops=16 * PAIRS * HD, bytes_accessed=4 << 20, transcendentals=0
        ),
        name="grads",
    )(*args)


def per_device(query, key_rows, value_rows, output, grad_out, block_order, segment):
    n = lax.axis_size("ctx")
    z_groups = [[z * 2 * YS + r for z in range(ZS)] for r in range(2 * YS)]
    y_groups = [
        [z * 2 * YS + y * 2 + c for y in range(YS)] for z in range(ZS) for c in range(2)
    ]

    def swap(x, bits):
        return lax.ppermute(x, "ctx", [(i, i ^ bits) for i in range(n)])

    def exchange(x, groups):
        return lax.all_to_all(x, "ctx", 0, 0, tiled=True, axis_index_groups=groups)

    kv_pay, q_pay, g_pay = pack(
        block_order, segment.reshape(1, TOK), query, key_rows, value_rows, output, grad_out
    )
    kv_own = exchange(kv_pay, z_groups)
    q_far, q_near = swap(q_pay, 4), swap(q_pay, 2)
    g_far, g_near = swap(g_pay, 4), swap(g_pay, 2)
    queries = [q_pay, q_near, q_far, swap(q_far, 2)]
    outs = [g_pay, g_near, g_far, swap(g_far, 2)]
    kv_own, queries, outs = lax.optimization_barrier((kv_own, queries, outs))
    kv_twin = swap(kv_own, 1)
    p_own, st_own = scores(kv_own, queries)
    y_index = (lax.axis_index("ctx") // 2 % YS).astype(jnp.int32).reshape(1)
    p_twin, st_twin, stats = scores(kv_twin, queries, st_own, y_index)
    all_stats = exchange(stats, y_groups)
    dkv_twin, dq = grads(kv_twin, p_twin, st_twin, all_stats, queries, outs)
    dkv_back = swap(dkv_twin, 1)
    dkv_own, dq_own, *dq_send = grads(kv_own, p_own, st_own, all_stats, queries, outs, dq)
    dkv = (dkv_own + dkv_back.astype(F32)).astype(BF16)
    dkv_all = exchange(dkv, z_groups)
    dq_parts = [swap(part, 2 * x) for x, part in enumerate(dq_send, 1)]
    grad_query = dq_own + sum(part.astype(F32) for part in dq_parts)
    grad_kv = jnp.sum(dkv_all.astype(F32), axis=0).astype(BF16)
    return grad_query.astype(BF16), grad_kv[:, 0:HD], grad_kv[:, HD : 2 * HD]


def solution(mesh):
    both = P("ctx", "kvh")
    return jax.shard_map(
        per_device,
        mesh=mesh,
        in_specs=(both, both, both, both, both, P("ctx"), P("ctx")),
        out_specs=(both, both, both),
        check_vma=False,
    )
```

```python
import functools

import jax
import jax.numpy as jnp
from jax import lax
from jax.experimental import pallas as pl
from jax.experimental.pallas import tpu as pltpu
from jax.sharding import PartitionSpec as P

HEADS = 32
KV_HEADS = 8
HD = 128
GROUP = HEADS // KV_HEADS
BLK = 64
TOKENS = 8192
TOK = 128
EXTRA = 16
PAY = TOK + EXTRA
YS = 4
ZS = 8
QT = YS * TOK
KT = 2 * TOK
SCALE = HD**-0.5
EXP2 = SCALE * 1.4426950408889634
MASKED = -1e30
FLOOR = -1e25
F32 = jnp.float32
BF16 = jnp.bfloat16
VMEM_LIMIT = 24

NT = (((1,), (1,)), ((), ()))
TN = (((0,), (0,)), ((), ()))


def dot(a, b, dims=(((1,), (0,)), ((), ()))):
    return lax.dot_general(a, b, dims, preferred_element_type=F32)


def pack_kernel(
    order_hbm, seg_hbm, q_hbm, k_hbm, v_hbm, o_hbm, g_hbm, kvp_hbm, qp_ref, gp_ref,
    order_ref, seg_ref, kv_ref, o_ref, in_sems, out_sems,
):
    moves = (
        (order_hbm, order_ref),
        (seg_hbm, seg_ref),
        (k_hbm, kv_ref.at[0:TOK, 0:HD]),
        (v_hbm, kv_ref.at[0:TOK, HD : 2 * HD]),
        (q_hbm, qp_ref.at[0:TOK]),
        (g_hbm, gp_ref.at[0:TOK]),
        (o_hbm, o_ref),
    )
    copies = [
        pltpu.make_async_copy(src, dst, in_sems.at[i]) for i, (src, dst) in enumerate(moves)
    ]
    for copy in copies:
        copy.start()
    for copy in copies[:4]:
        copy.wait()
    lane = lax.broadcasted_iota(jnp.int32, (1, TOK), 1)
    block = jnp.where(lane < BLK, order_ref[0], order_ref[1]).astype(F32)
    doc = seg_ref[...].astype(F32)
    kv_extra = jnp.concatenate([doc, block], axis=1)
    kv_ref[TOK:PAY, :] = jnp.broadcast_to(kv_extra, (EXTRA, 2 * HD)).astype(BF16)
    outs = [
        pltpu.make_async_copy(kv_ref, kvp_hbm.at[z], out_sems.at[z]) for z in range(ZS)
    ]
    for copy in outs:
        copy.start()
    for copy in copies[4:]:
        copy.wait()
    highs, lows = [], []
    for h in range(GROUP):
        cols = slice(h * HD, (h + 1) * HD)
        prod = gp_ref[0:TOK, cols].astype(F32) * o_ref[:, cols].astype(F32)
        delta = jnp.sum(prod.T, axis=0, keepdims=True)
        high = delta.astype(BF16).astype(F32)
        highs.append(high)
        lows.append(delta - high)
    zero = jnp.zeros_like(doc)
    q_extra = jnp.concatenate([doc, block, zero, zero], axis=1)
    qp_ref[TOK:PAY, :] = jnp.broadcast_to(q_extra, (EXTRA, GROUP * HD)).astype(BF16)
    row = lax.broadcasted_iota(jnp.int32, (EXTRA, GROUP * HD), 0)
    g_extra = jnp.where(
        row == 0, jnp.concatenate(highs, axis=1), jnp.concatenate(lows, axis=1)
    )
    gp_ref[TOK:PAY, :] = g_extra.astype(BF16)
    for copy in outs:
        copy.wait()


def code_of(doc, block):
    lane = lax.broadcasted_iota(jnp.int32, doc.shape, 1)
    within = jnp.where(lane < BLK, lane, lane - BLK).astype(F32)
    return doc * TOKENS + block * BLK + within


def score_kernel(n_prev, *refs):
    kv_ref, *rest = refs
    q_refs, rest = rest[:YS], rest[YS:]
    if n_prev:
        y_ref, prev_ref, pt_ref, st_ref, fin_ref, qs, code, bias, keep = rest
    else:
        pt_ref, st_ref, qs, code, bias = rest
    step = pl.program_id(0)

    @pl.when(step == 0)
    def _():
        for x, q_ref in enumerate(q_refs):
            toks = slice(x * TOK, (x + 1) * TOK)
            for h in range(GROUP):
                qs[h, toks, :] = q_ref[0:TOK, h * HD : (h + 1) * HD]
            info = q_ref[TOK:PAY, :].astype(F32)
            doc, block = info[0:1, 0:TOK], info[0:1, TOK : 2 * TOK]
            code[0:1, toks] = code_of(doc, block)
            code[1:2, toks] = doc * TOKENS

    for b in range(2):
        info = kv_ref[b, TOK:PAY, :].astype(F32)
        key_code = code_of(info[0:1, 0:TOK], info[0:1, TOK : 2 * TOK])
        key_code = jnp.broadcast_to(key_code, (TOK, TOK)).T
        for x in range(YS):
            toks = slice(x * TOK, (x + 1) * TOK)
            ok = (key_code <= code[0:1, toks]) & (key_code >= code[1:2, toks])
            bias[b * TOK : (b + 1) * TOK, toks] = jnp.where(ok, 0.0, MASKED)
    keys = jnp.concatenate([kv_ref[0, 0:TOK, 0:HD], kv_ref[1, 0:TOK, 0:HD]], axis=0)
    for h in range(GROUP):
        s = dot(keys, qs[h], NT) + bias[...]
        peak = jnp.maximum(jnp.max(s, axis=0, keepdims=True), FLOOR)
        p = jnp.exp2((s - peak) * EXP2)
        st_ref[0, h : h + 1, :] = peak
        st_ref[0, GROUP + h : GROUP + h + 1, :] = jnp.sum(p, axis=0, keepdims=True)
        pt_ref[:, h * QT : (h + 1) * QT] = p.astype(BF16)
    if n_prev:
        keep[pl.ds(step, 1)] = st_ref[...]

        @pl.when(step == pl.num_programs(0) - 1)
        def _():
            tiles = [prev_ref[t] for t in range(n_prev)] + [keep[t] for t in range(n_prev)]
            top = functools.reduce(jnp.maximum, [t[0:GROUP] for t in tiles])
            total = sum(t[GROUP:] * jnp.exp2((t[0:GROUP] - top) * EXP2) for t in tiles)
            for d in range(YS):
                for x in range(YS):
                    to, of = slice(x * TOK, (x + 1) * TOK), slice((x ^ d) * TOK, ((x ^ d) + 1) * TOK)
                    fin_ref[y_ref[0] ^ d, 0:GROUP, to] = top[:, of]
                    fin_ref[y_ref[0] ^ d, GROUP : 2 * GROUP, to] = total[:, of]


def grad_kernel(last, kv_ref, pt_ref, st_ref, all_ref, *rest):
    q_refs, g_refs, rest = rest[:YS], rest[YS : 2 * YS], rest[2 * YS :]
    if last:
        dq_in, dkv_ref, own_ref, send1, send2, send3, qs, gs, delta, dq = rest
    else:
        dkv_ref, dq, qs, gs, delta = rest
    step = pl.program_id(0)

    @pl.when(step == 0)
    def _():
        for x, (q_ref, g_ref) in enumerate(zip(q_refs, g_refs)):
            toks = slice(x * TOK, (x + 1) * TOK)
            info = g_ref[TOK:PAY, :].astype(F32)
            for h in range(GROUP):
                cols = slice(h * HD, (h + 1) * HD)
                qs[h, toks, :] = q_ref[0:TOK, cols]
                gs[h, toks, :] = g_ref[0:TOK, cols]
                delta[h : h + 1, toks] = info[0:1, cols] + info[1:2, cols]
        dq[...] = dq_in[...] if last else jnp.zeros_like(dq)

    top = functools.reduce(jnp.maximum, [all_ref[y, 0:GROUP] for y in range(YS)])
    total = sum(
        all_ref[y, GROUP : 2 * GROUP] * jnp.exp2((all_ref[y, 0:GROUP] - top) * EXP2)
        for y in range(YS)
    )
    weight = jnp.exp2((st_ref[0, 0:GROUP] - top) * EXP2) / total
    keys = jnp.concatenate([kv_ref[0, 0:TOK, 0:HD], kv_ref[1, 0:TOK, 0:HD]], axis=0)
    values = jnp.concatenate(
        [kv_ref[0, 0:TOK, HD : 2 * HD], kv_ref[1, 0:TOK, HD : 2 * HD]], axis=0
    )
    dk = jnp.zeros((KT, HD), F32)
    dv = jnp.zeros((KT, HD), F32)
    for h in range(GROUP):
        dp = dot(values, gs[h], NT)
        p = pt_ref[:, h * QT : (h + 1) * QT].astype(F32) * weight[h : h + 1]
        ds = (p * (dp - delta[h : h + 1, :])).astype(BF16)
        dv = dv + dot(p.astype(BF16), gs[h])
        dk = dk + dot(ds, qs[h])
        dq[h] += dot(keys, ds, TN)
    dk = dk * SCALE
    for b in range(2):
        rows = slice(b * TOK, (b + 1) * TOK)
        dkv_ref[b, :, 0:HD] = dk[rows].astype(dkv_ref.dtype)
        dkv_ref[b, :, HD : 2 * HD] = dv[rows].astype(dkv_ref.dtype)

    if last:

        @pl.when(step == pl.num_programs(0) - 1)
        def _():
            for x, out in enumerate((own_ref, send1, send2, send3)):
                for h in range(GROUP):
                    part = dq[h, :, x * TOK : (x + 1) * TOK].T * SCALE
                    out[:, h * HD : (h + 1) * HD] = part.astype(out.dtype)


def whole(shape):
    return pl.BlockSpec(shape, lambda *_: (0,) * len(shape))


def shape_of(shape, dtype):
    return jax.ShapeDtypeStruct(shape, dtype)


def params(limit=VMEM_LIMIT):
    return pltpu.CompilerParams(vmem_limit_bytes=limit << 20)


def pack(order, seg, q, k, v, o, g):
    hbm = pl.BlockSpec(memory_space=pltpu.HBM)
    vm = pl.BlockSpec(memory_space=pltpu.VMEM)
    pay = shape_of((PAY, GROUP * HD), BF16)
    return pl.pallas_call(
        pack_kernel,
        out_shape=(shape_of((ZS, PAY, 2 * HD), BF16), pay, pay),
        in_specs=[hbm] * 7,
        out_specs=(hbm, vm, vm),
        scratch_shapes=[
            pltpu.SMEM((2,), jnp.int32),
            pltpu.VMEM((1, TOK), jnp.int32),
            pltpu.VMEM((PAY, 2 * HD), BF16),
            pltpu.VMEM((TOK, GROUP * HD), BF16),
            pltpu.SemaphoreType.DMA((7,)),
            pltpu.SemaphoreType.DMA((ZS,)),
        ],
        compiler_params=params(60),
        name="pack",
    )(order, seg, q, k, v, o, g)


STEPS = ZS // 2
PAIRS = ZS * TOK * GROUP * QT


def scores(kv, queries, prev=None, y_index=None):
    in_specs = [pl.BlockSpec((2, PAY, 2 * HD), lambda i: (i, 0, 0))]
    in_specs += [whole((PAY, GROUP * HD))] * YS
    args = [kv, *queries]
    out_shape = [
        shape_of((ZS * TOK, GROUP * QT), BF16),
        shape_of((STEPS, 2 * GROUP, QT), F32),
    ]
    out_specs = [
        pl.BlockSpec((KT, GROUP * QT), lambda i: (i, 0)),
        pl.BlockSpec((1, 2 * GROUP, QT), lambda i: (i, 0, 0)),
    ]
    scratch = [
        pltpu.VMEM((GROUP, QT, HD), BF16),
        pltpu.VMEM((8, QT), F32),
        pltpu.VMEM((KT, QT), F32),
    ]
    if prev is not None:
        in_specs += [pl.BlockSpec(memory_space=pltpu.SMEM), whole(prev.shape)]
        args += [y_index, prev]
        out_shape.append(shape_of((YS, 2 * GROUP, QT), F32))
        out_specs.append(whole((YS, 2 * GROUP, QT)))
        scratch.append(pltpu.VMEM((STEPS, 2 * GROUP, QT), F32))
    return pl.pallas_call(
        functools.partial(score_kernel, 0 if prev is None else STEPS),
        grid=(STEPS,),
        in_specs=in_specs,
        out_specs=out_specs,
        out_shape=out_shape,
        scratch_shapes=scratch,
        compiler_params=params(),
        cost_estimate=pl.CostEstimate(
            flops=PAIRS, bytes_accessed=1 << 16, transcendentals=0
        ),
        name="scores",
    )(*args)


def grads(kv, probs, stats, all_stats, queries, outs, dq_in=None):
    last = dq_in is not None
    in_specs = [
        pl.BlockSpec((2, PAY, 2 * HD), lambda i: (i, 0, 0)),
        pl.BlockSpec((KT, GROUP * QT), lambda i: (i, 0)),
        pl.BlockSpec((1, 2 * GROUP, QT), lambda i: (i, 0, 0)),
        whole((YS, 2 * GROUP, QT)),
    ] + [whole((PAY, GROUP * HD))] * (2 * YS)
    args = [kv, probs, stats, all_stats, *queries, *outs]
    dkv_type = F32 if last else BF16
    out_shape = [shape_of((ZS, TOK, 2 * HD), dkv_type)]
    out_specs = [pl.BlockSpec((2, TOK, 2 * HD), lambda i: (i, 0, 0))]
    dq_shape = (GROUP, HD, QT)
    scratch = [
        pltpu.VMEM((GROUP, QT, HD), BF16),
        pltpu.VMEM((GROUP, QT, HD), BF16),
        pltpu.VMEM((8, QT), F32),
    ]
    if last:
        in_specs.append(whole(dq_shape))
        args.append(dq_in)
        out_shape += [shape_of((TOK, GROUP * HD), F32)]
        out_shape += [shape_of((TOK, GROUP * HD), BF16)] * (YS - 1)
        out_specs += [whole((TOK, GROUP * HD))] * YS
        scratch.append(pltpu.VMEM(dq_shape, F32))
    else:
        out_shape.append(shape_of(dq_shape, F32))
        out_specs.append(whole(dq_shape))
    return pl.pallas_call(
        functools.partial(grad_kernel, last),
        grid=(STEPS,),
        in_specs=in_specs,
        out_specs=out_specs,
        out_shape=out_shape,
        scratch_shapes=scratch,
        compiler_params=params(),
        cost_estimate=pl.CostEstimate(
            flops=16 * PAIRS * HD, bytes_accessed=4 << 20, transcendentals=0
        ),
        name="grads",
    )(*args)


def per_device(query, key_rows, value_rows, output, grad_out, block_order, segment):
    n = lax.axis_size("ctx")
    z_groups = [[z * 2 * YS + r for z in range(ZS)] for r in range(2 * YS)]
    y_groups = [
        [z * 2 * YS + y * 2 + c for y in range(YS)] for z in range(ZS) for c in range(2)
    ]

    def swap(x, bits):
        return lax.ppermute(x, "ctx", [(i, i ^ bits) for i in range(n)])

    def exchange(x, groups):
        return lax.all_to_all(x, "ctx", 0, 0, tiled=True, axis_index_groups=groups)

    kv_pay, q_pay, g_pay = pack(
        block_order, segment.reshape(1, TOK), query, key_rows, value_rows, output, grad_out
    )
    kv_own = exchange(kv_pay, z_groups)
    q_far, q_near = swap(q_pay, 4), swap(q_pay, 2)
    g_far, g_near = swap(g_pay, 4), swap(g_pay, 2)
    queries = [q_pay, q_near, q_far, swap(q_far, 2)]
    outs = [g_pay, g_near, g_far, swap(g_far, 2)]
    kv_own, queries, outs = lax.optimization_barrier((kv_own, queries, outs))
    kv_twin = swap(kv_own, 1)
    p_own, st_own = scores(kv_own, queries)
    y_index = (lax.axis_index("ctx") // 2 % YS).astype(jnp.int32).reshape(1)
    p_twin, st_twin, stats = scores(kv_twin, queries, st_own, y_index)
    all_stats = exchange(stats, y_groups)
    dkv_twin, dq = grads(kv_twin, p_twin, st_twin, all_stats, queries, outs)
    dkv_back = swap(dkv_twin, 1)
    dkv_own, dq_own, *dq_send = grads(kv_own, p_own, st_own, all_stats, queries, outs, dq)
    dkv = (dkv_own + dkv_back.astype(F32)).astype(BF16)
    dkv_all = exchange(dkv, z_groups)
    dq_parts = [swap(part, 2 * x) for x, part in enumerate(dq_send, 1)]
    grad_query = dq_own + sum(part.astype(F32) for part in dq_parts)
    grad_kv = jnp.sum(dkv_all.astype(F32), axis=0).astype(BF16)
    return grad_query.astype(BF16), grad_kv[:, 0:HD], grad_kv[:, HD : 2 * HD]


def solution(mesh):
    both = P("ctx", "kvh")
    return jax.shard_map(
        per_device,
        mesh=mesh,
        in_specs=(both, both, both, both, both, P("ctx"), P("ctx")),
        out_specs=(both, both, both),
        check_vma=False,
    )
```

```python
import functools

import jax
import jax.numpy as jnp
from jax import lax
from jax.experimental import pallas as pl
from jax.experimental.pallas import tpu as pltpu
from jax.sharding import PartitionSpec as P

HEADS = 32
KV_HEADS = 8
HD = 128
GROUP = HEADS // KV_HEADS
BLK = 64
TOKENS = 8192
TOK = 128
EXTRA = 16
PAY = TOK + EXTRA
YS = 4
ZS = 8
QT = YS * TOK
KT = 2 * TOK
SCALE = HD**-0.5
EXP2 = SCALE * 1.4426950408889634
MASKED = -1e30
FLOOR = -1e25
F32 = jnp.float32
BF16 = jnp.bfloat16
VMEM_LIMIT = 24
PAIR_LIMIT = 46

NT = (((1,), (1,)), ((), ()))
TN = (((0,), (0,)), ((), ()))


def dot(a, b, dims=(((1,), (0,)), ((), ()))):
    return lax.dot_general(a, b, dims, preferred_element_type=F32)


def pack_kernel(
    order_hbm, seg_hbm, q_hbm, k_hbm, v_hbm, o_hbm, g_hbm, kvp_hbm, qp_ref, gp_ref,
    order_ref, seg_ref, kv_ref, o_ref, in_sems, out_sems,
):
    moves = (
        (order_hbm, order_ref),
        (seg_hbm, seg_ref),
        (k_hbm, kv_ref.at[0:TOK, 0:HD]),
        (v_hbm, kv_ref.at[0:TOK, HD : 2 * HD]),
        (q_hbm, qp_ref.at[0:TOK]),
        (g_hbm, gp_ref.at[0:TOK]),
        (o_hbm, o_ref),
    )
    copies = [
        pltpu.make_async_copy(src, dst, in_sems.at[i]) for i, (src, dst) in enumerate(moves)
    ]
    for copy in copies:
        copy.start()
    for copy in copies[:4]:
        copy.wait()
    lane = lax.broadcasted_iota(jnp.int32, (1, TOK), 1)
    block = jnp.where(lane < BLK, order_ref[0], order_ref[1]).astype(F32)
    doc = seg_ref[...].astype(F32)
    kv_extra = jnp.concatenate([doc, block], axis=1)
    kv_ref[TOK:PAY, :] = jnp.broadcast_to(kv_extra, (EXTRA, 2 * HD)).astype(BF16)
    outs = [
        pltpu.make_async_copy(kv_ref, kvp_hbm.at[z], out_sems.at[z]) for z in range(ZS)
    ]
    for copy in outs:
        copy.start()
    for copy in copies[4:]:
        copy.wait()
    highs, lows = [], []
    for h in range(GROUP):
        cols = slice(h * HD, (h + 1) * HD)
        prod = gp_ref[0:TOK, cols].astype(F32) * o_ref[:, cols].astype(F32)
        delta = jnp.sum(prod.T, axis=0, keepdims=True)
        high = delta.astype(BF16).astype(F32)
        highs.append(high)
        lows.append(delta - high)
    zero = jnp.zeros_like(doc)
    q_extra = jnp.concatenate([doc, block, zero, zero], axis=1)
    qp_ref[TOK:PAY, :] = jnp.broadcast_to(q_extra, (EXTRA, GROUP * HD)).astype(BF16)
    row = lax.broadcasted_iota(jnp.int32, (EXTRA, GROUP * HD), 0)
    g_extra = jnp.where(
        row == 0, jnp.concatenate(highs, axis=1), jnp.concatenate(lows, axis=1)
    )
    gp_ref[TOK:PAY, :] = g_extra.astype(BF16)
    for copy in outs:
        copy.wait()


def code_of(doc, block):
    lane = lax.broadcasted_iota(jnp.int32, doc.shape, 1)
    within = jnp.where(lane < BLK, lane, lane - BLK).astype(F32)
    return doc * TOKENS + block * BLK + within


def load_queries(q_refs, qs, code):
    for x, q_ref in enumerate(q_refs):
        toks = slice(x * TOK, (x + 1) * TOK)
        for h in range(GROUP):
            qs[h, toks, :] = q_ref[0:TOK, h * HD : (h + 1) * HD]
        info = q_ref[TOK:PAY, :].astype(F32)
        doc, block = info[0:1, 0:TOK], info[0:1, TOK : 2 * TOK]
        code[0:1, toks] = code_of(doc, block)
        code[1:2, toks] = doc * TOKENS


def fill_bias(kv_ref, code, bias):
    for b in range(2):
        info = kv_ref[b, TOK:PAY, :].astype(F32)
        key_code = code_of(info[0:1, 0:TOK], info[0:1, TOK : 2 * TOK])
        key_code = jnp.broadcast_to(key_code, (TOK, TOK)).T
        for x in range(YS):
            toks = slice(x * TOK, (x + 1) * TOK)
            ok = (key_code <= code[0:1, toks]) & (key_code >= code[1:2, toks])
            bias[b * TOK : (b + 1) * TOK, toks] = jnp.where(ok, 0.0, MASKED)


def score_kernel(last, kv_ref, *rest):
    q_refs, rest = rest[:YS], rest[YS:]
    if last:
        y_ref, prev_ref, send_ref, mine_ref, qs, code, bias, keep = rest
    else:
        st_ref, qs, code, bias = rest
    step = pl.program_id(0)

    @pl.when(step == 0)
    def _():
        load_queries(q_refs, qs, code)

    fill_bias(kv_ref, code, bias)
    keys = jnp.concatenate([kv_ref[0, 0:TOK, 0:HD], kv_ref[1, 0:TOK, 0:HD]], axis=0)
    peaks, totals = [], []
    for h in range(GROUP):
        s = dot(keys, qs[h], NT) + bias[...]
        peak = jnp.maximum(jnp.max(s, axis=0, keepdims=True), FLOOR)
        peaks.append(peak)
        totals.append(jnp.sum(jnp.exp2((s - peak) * EXP2), axis=0, keepdims=True))
    stats = jnp.concatenate(peaks + totals, axis=0)
    if not last:
        st_ref[0] = stats
        return
    keep[pl.ds(step, 1)] = stats[None]

    @pl.when(step == STEPS - 1)
    def _():
        tiles = [ref[t] for ref in (prev_ref, keep) for t in range(STEPS)]
        top = functools.reduce(jnp.maximum, [t[0:GROUP] for t in tiles])
        total = sum(t[GROUP:] * jnp.exp2((t[0:GROUP] - top) * EXP2) for t in tiles)
        mine_ref[0:GROUP, :] = top
        mine_ref[GROUP : 2 * GROUP, :] = total
        for d in range(YS):
            for x in range(YS):
                to, of = slice(x * TOK, (x + 1) * TOK), slice((x ^ d) * TOK, ((x ^ d) + 1) * TOK)
                send_ref[y_ref[0] ^ d, 0:GROUP, to] = top[:, of]
                send_ref[y_ref[0] ^ d, GROUP : 2 * GROUP, to] = total[:, of]


def pair_kernel(own_ref, twin_ref, mine_ref, *rest):
    q_refs, g_refs, rest = rest[:YS], rest[YS : 2 * YS], rest[2 * YS :]
    pds_ref, dq_own, dq1, dq2, dq3, kv, qs, gs, code, delta, bias, dq = rest
    step = pl.program_id(0)

    @pl.when(step == 0)
    def _():
        load_queries(q_refs, qs, code)
        for x, g_ref in enumerate(g_refs):
            toks = slice(x * TOK, (x + 1) * TOK)
            info = g_ref[TOK:PAY, :].astype(F32)
            for h in range(GROUP):
                cols = slice(h * HD, (h + 1) * HD)
                gs[h, toks, :] = g_ref[0:TOK, cols]
                delta[h : h + 1, toks] = info[0:1, cols] + info[1:2, cols]
        dq[...] = jnp.zeros_like(dq)

    @pl.when(step < STEPS)
    def _():
        kv[...] = own_ref[...]

    @pl.when(step >= STEPS)
    def _():
        kv[...] = twin_ref[...]

    fill_bias(kv, code, bias)
    keys = jnp.concatenate([kv[0, 0:TOK, 0:HD], kv[1, 0:TOK, 0:HD]], axis=0)
    values = jnp.concatenate([kv[0, 0:TOK, HD : 2 * HD], kv[1, 0:TOK, HD : 2 * HD]], axis=0)
    for h in range(GROUP):
        s = dot(keys, qs[h], NT) + bias[...]
        p = jnp.exp2((s - mine_ref[h : h + 1, :]) * EXP2)
        dp = dot(values, gs[h], NT)
        ds = (p * (dp - delta[h : h + 1, :])).astype(BF16)
        pds_ref[:, h * QT : (h + 1) * QT] = p.astype(BF16)
        pds_ref[:, (GROUP + h) * QT : (GROUP + h + 1) * QT] = ds
        dq[h] += dot(keys, ds, TN)

    @pl.when(step == 2 * STEPS - 1)
    def _():
        for x, out in enumerate((dq_own, dq1, dq2, dq3)):
            for h in range(GROUP):
                part = dq[h, :, x * TOK : (x + 1) * TOK].T * SCALE
                out[:, h * HD : (h + 1) * HD] = part.astype(out.dtype)


def columns(rows):
    rows = jnp.concatenate(rows, axis=0)
    pad = jnp.zeros((TOK - rows.shape[0], TOK), F32)
    return jnp.concatenate([rows, pad], axis=0).T


def weigh(all_ref, mine_ref, y_ref, q_refs, g_refs, qw, gw, back_ref):
    top = functools.reduce(jnp.maximum, [all_ref[y, 0:GROUP] for y in range(YS)])
    total = sum(
        all_ref[y, GROUP : 2 * GROUP] * jnp.exp2((all_ref[y, 0:GROUP] - top) * EXP2)
        for y in range(YS)
    )
    mine = jnp.exp2((mine_ref[0:GROUP] - top) * EXP2) / total
    pieces = [(h, x) for h in range(GROUP) for x in range(YS)]
    weights = columns([mine[h : h + 1, x * TOK : (x + 1) * TOK] for h, x in pieces])
    for i, (h, x) in enumerate(pieces):
        cols, toks = slice(h * HD, (h + 1) * HD), slice(h * QT + x * TOK, h * QT + (x + 1) * TOK)
        weight = jnp.broadcast_to(weights[:, i : i + 1], (TOK, HD))
        qw[toks, :] = (q_refs[x][0:TOK, cols].astype(F32) * (weight * SCALE)).astype(BF16)
        gw[toks, :] = (g_refs[x][0:TOK, cols].astype(F32) * weight).astype(BF16)
    rows = []
    for x in range(YS):
        peak = all_ref[y_ref[0] ^ x, 0:GROUP, 0:TOK]
        back = jnp.exp2((peak - top[:, 0:TOK]) * EXP2) / total[:, 0:TOK]
        rows += [back[h : h + 1] for h in range(GROUP)]
    back_ref[...] = columns(rows)


def key_kernel(first, pds_ref, *rest):
    if first:
        all_ref, mine_ref, y_ref, *rest = rest
        q_refs, g_refs, rest = rest[:YS], rest[YS : 2 * YS], rest[2 * YS :]
        dkv_ref, qw, gw, back_ref = rest

        @pl.when(pl.program_id(0) == 0)
        def _():
            weigh(all_ref, mine_ref, y_ref, q_refs, g_refs, qw, gw, back_ref)
    else:
        qw, gw, dkv_ref = rest
    dv = dot(pds_ref[:, 0 : GROUP * QT], gw[...])
    dk = dot(pds_ref[:, GROUP * QT : 2 * GROUP * QT], qw[...])
    for b in range(2):
        rows = slice(b * TOK, (b + 1) * TOK)
        dkv_ref[b, :, 0:HD] = dk[rows].astype(dkv_ref.dtype)
        dkv_ref[b, :, HD : 2 * HD] = dv[rows].astype(dkv_ref.dtype)


def sum_kernel(back_ref, p0, p1, p2, p3, out_ref):
    for h in range(GROUP):
        cols = slice(h * HD, (h + 1) * HD)
        total = jnp.zeros((TOK, HD), F32)
        for x, part in enumerate((p0, p1, p2, p3)):
            i = x * GROUP + h
            weight = jnp.broadcast_to(back_ref[:, i : i + 1], (TOK, HD))
            total = total + part[:, cols].astype(F32) * weight
        out_ref[:, cols] = total.astype(BF16)


def whole(shape):
    return pl.BlockSpec(shape, lambda *_: (0,) * len(shape))


def shape_of(shape, dtype):
    return jax.ShapeDtypeStruct(shape, dtype)


def params(limit=VMEM_LIMIT):
    return pltpu.CompilerParams(vmem_limit_bytes=limit << 20)


def pack(order, seg, q, k, v, o, g):
    hbm = pl.BlockSpec(memory_space=pltpu.HBM)
    vm = pl.BlockSpec(memory_space=pltpu.VMEM)
    pay = shape_of((PAY, GROUP * HD), BF16)
    return pl.pallas_call(
        pack_kernel,
        out_shape=(shape_of((ZS, PAY, 2 * HD), BF16), pay, pay),
        in_specs=[hbm] * 7,
        out_specs=(hbm, vm, vm),
        scratch_shapes=[
            pltpu.SMEM((2,), jnp.int32),
            pltpu.VMEM((1, TOK), jnp.int32),
            pltpu.VMEM((PAY, 2 * HD), BF16),
            pltpu.VMEM((TOK, GROUP * HD), BF16),
            pltpu.SemaphoreType.DMA((7,)),
            pltpu.SemaphoreType.DMA((ZS,)),
        ],
        compiler_params=params(60),
        name="pack",
    )(order, seg, q, k, v, o, g)


STEPS = ZS // 2
PAIRS = ZS * TOK * GROUP * QT
SMEM = pl.BlockSpec(memory_space=pltpu.SMEM)
PAYS = [whole((PAY, GROUP * HD))] * YS
STATS = (2 * GROUP, QT)


def cost(flops):
    return pl.CostEstimate(flops=flops, bytes_accessed=1 << 16, transcendentals=0)


def scores(kv, queries, prev=None, y_index=None):
    in_specs = [pl.BlockSpec((2, PAY, 2 * HD), lambda i: (i, 0, 0)), *PAYS]
    args = [kv, *queries]
    scratch = [
        pltpu.VMEM((GROUP, QT, HD), BF16),
        pltpu.VMEM((8, QT), F32),
        pltpu.VMEM((KT, QT), F32),
    ]
    if prev is None:
        out_shape = shape_of((STEPS, *STATS), F32)
        out_specs = pl.BlockSpec((1, *STATS), lambda i: (i, 0, 0))
    else:
        in_specs += [SMEM, whole(prev.shape)]
        args += [y_index, prev]
        out_shape = (shape_of((YS, *STATS), F32), shape_of(STATS, F32))
        out_specs = (whole((YS, *STATS)), whole(STATS))
        scratch.append(pltpu.VMEM((STEPS, *STATS), F32))
    return pl.pallas_call(
        functools.partial(score_kernel, prev is not None),
        grid=(STEPS,),
        in_specs=in_specs,
        out_specs=out_specs,
        out_shape=out_shape,
        scratch_shapes=scratch,
        compiler_params=params(),
        cost_estimate=cost(PAIRS),
        name="scores",
    )(*args)


def pairs(kv_own, kv_twin, mine, queries, outs):
    dq_spec = whole((TOK, GROUP * HD))
    return pl.pallas_call(
        pair_kernel,
        grid=(2 * STEPS,),
        in_specs=[
            pl.BlockSpec((2, PAY, 2 * HD), lambda i: (jnp.minimum(i, STEPS - 1), 0, 0)),
            pl.BlockSpec((2, PAY, 2 * HD), lambda i: (jnp.maximum(i - STEPS, 0), 0, 0)),
            whole(STATS),
            *PAYS,
            *PAYS,
        ],
        out_specs=[pl.BlockSpec((KT, 2 * GROUP * QT), lambda i: (i, 0))] + [dq_spec] * YS,
        out_shape=[
            shape_of((2 * ZS * TOK, 2 * GROUP * QT), BF16),
            shape_of((TOK, GROUP * HD), F32),
        ]
        + [shape_of((TOK, GROUP * HD), BF16)] * (YS - 1),
        scratch_shapes=[
            pltpu.VMEM((2, PAY, 2 * HD), BF16),
            pltpu.VMEM((GROUP, QT, HD), BF16),
            pltpu.VMEM((GROUP, QT, HD), BF16),
            pltpu.VMEM((8, QT), F32),
            pltpu.VMEM((8, QT), F32),
            pltpu.VMEM((KT, QT), F32),
            pltpu.VMEM((GROUP, HD, QT), F32),
        ],
        compiler_params=params(PAIR_LIMIT),
        cost_estimate=cost(12 * PAIRS * HD),
        name="pairs",
    )(kv_own, kv_twin, mine, *queries, *outs)


def key_grads(pds, half, dtype, first=None, weighted=None):
    in_specs = [pl.BlockSpec((KT, 2 * GROUP * QT), lambda i: (i + half * STEPS, 0))]
    rows = (GROUP * QT, HD)
    out_shape = [shape_of((ZS, TOK, 2 * HD), dtype)]
    out_specs = [pl.BlockSpec((2, TOK, 2 * HD), lambda i: (i, 0, 0))]
    if first:
        all_stats, mine, y_index, queries, outs = first
        in_specs += [whole((YS, *STATS)), whole(STATS), SMEM, *PAYS, *PAYS]
        args = [all_stats, mine, y_index, *queries, *outs]
        out_shape += [shape_of(rows, BF16)] * 2 + [shape_of((TOK, TOK), F32)]
        out_specs += [whole(rows)] * 2 + [whole((TOK, TOK))]
    else:
        in_specs += [whole(rows)] * 2
        args = weighted
    return pl.pallas_call(
        functools.partial(key_kernel, bool(first)),
        grid=(STEPS,),
        in_specs=in_specs,
        out_specs=out_specs,
        out_shape=out_shape,
        compiler_params=params(PAIR_LIMIT),
        cost_estimate=cost(2 * PAIRS * HD),
        name="key_grads",
    )(pds, *args)


def sum_queries(back, parts):
    vm = pl.BlockSpec(memory_space=pltpu.VMEM)
    return pl.pallas_call(
        sum_kernel,
        in_specs=[vm] * 5,
        out_specs=vm,
        out_shape=shape_of((TOK, GROUP * HD), BF16),
        compiler_params=params(),
        name="sum_queries",
    )(back, *parts)


def per_device(query, key_rows, value_rows, output, grad_out, block_order, segment):
    n = lax.axis_size("ctx")
    z_groups = [[z * 2 * YS + r for z in range(ZS)] for r in range(2 * YS)]
    y_groups = [
        [z * 2 * YS + y * 2 + c for y in range(YS)] for z in range(ZS) for c in range(2)
    ]

    def swap(x, bits):
        return lax.ppermute(x, "ctx", [(i, i ^ bits) for i in range(n)])

    def exchange(x, groups):
        return lax.all_to_all(x, "ctx", 0, 0, tiled=True, axis_index_groups=groups)

    kv_pay, q_pay, g_pay = pack(
        block_order, segment.reshape(1, TOK), query, key_rows, value_rows, output, grad_out
    )
    kv_own = exchange(kv_pay, z_groups)
    g_far, g_near = swap(g_pay, 4), swap(g_pay, 2)
    queries = [q_pay] + [swap(q_pay, 2 * x) for x in range(1, YS)]
    kv_own, queries, g_near, g_far = lax.optimization_barrier((kv_own, queries, g_near, g_far))
    kv_twin = swap(kv_own, 1)
    outs = [g_pay, g_near, g_far, swap(g_far, 2)]
    st_own = scores(kv_own, queries)
    kv_twin, outs = lax.optimization_barrier((kv_twin, outs))
    y_index = (lax.axis_index("ctx").astype(jnp.int32) >> 1 & (YS - 1)).reshape(1)
    send, mine = scores(kv_twin, queries, st_own, y_index)
    all_stats = exchange(send, y_groups)
    pds, *dq_parts = pairs(kv_own, kv_twin, mine, queries, outs)
    first = (all_stats, mine, y_index, queries, outs)
    dkv_twin, qw, gw, back = key_grads(pds, 1, BF16, first=first)
    dkv_back = swap(dkv_twin, 1)
    (dkv_own,) = key_grads(pds, 0, F32, weighted=(qw, gw))
    dkv = (dkv_own + dkv_back.astype(F32)).astype(BF16)
    dkv_all = exchange(dkv, z_groups)
    parts = [dq_parts[0]] + [swap(part, 2 * x) for x, part in enumerate(dq_parts[1:], 1)]
    grad_query = sum_queries(back, parts)
    grad_kv = jnp.sum(dkv_all.astype(F32), axis=0).astype(BF16)
    return grad_query, grad_kv[:, 0:HD], grad_kv[:, HD : 2 * HD]


def solution(mesh):
    both = P("ctx", "kvh")
    return jax.shard_map(
        per_device,
        mesh=mesh,
        in_specs=(both, both, both, both, both, P("ctx"), P("ctx")),
        out_specs=(both, both, both),
        check_vma=False,
    )
```

```python
import functools

import jax
import jax.numpy as jnp
from jax import lax
from jax.experimental import pallas as pl
from jax.experimental.pallas import tpu as pltpu
from jax.sharding import PartitionSpec as P

HEADS = 32
KV_HEADS = 8
HD = 128
GROUP = HEADS // KV_HEADS
BLK = 64
TOKENS = 8192
TOK = 128
EXTRA = 16
PAY = TOK + EXTRA
YS = 4
TILE = (0, 2, 8, 10)
ZS = 8
WIDE = GROUP * HD
QT = YS * TOK
KT = 2 * TOK
SCALE = HD**-0.5
EXP2 = SCALE * 1.4426950408889634
MASKED = -1e30
FLOOR = -1e25
F32 = jnp.float32
BF16 = jnp.bfloat16
VMEM_LIMIT = 24

NT = (((1,), (1,)), ((), ()))
TN = (((0,), (0,)), ((), ()))


def dot(a, b, dims=(((1,), (0,)), ((), ()))):
    return lax.dot_general(a, b, dims, preferred_element_type=F32)


def pack_kernel(
    order_hbm, seg_hbm, q_hbm, k_hbm, v_hbm, o_hbm, g_hbm, kvp_hbm, qp_ref,
    order_ref, seg_ref, kv_ref, o_ref, in_sems, out_sems,
):
    moves = (
        (order_hbm, order_ref),
        (seg_hbm, seg_ref),
        (k_hbm, kv_ref.at[0:TOK, 0:HD]),
        (v_hbm, kv_ref.at[0:TOK, HD : 2 * HD]),
        (q_hbm, qp_ref.at[0:TOK, 0:WIDE]),
        (g_hbm, qp_ref.at[0:TOK, WIDE : 2 * WIDE]),
        (o_hbm, o_ref),
    )
    copies = [
        pltpu.make_async_copy(src, dst, in_sems.at[i]) for i, (src, dst) in enumerate(moves)
    ]
    for copy in copies:
        copy.start()
    for copy in copies[:4]:
        copy.wait()
    lane = lax.broadcasted_iota(jnp.int32, (1, TOK), 1)
    block = jnp.where(lane < BLK, order_ref[0], order_ref[1]).astype(F32)
    doc = seg_ref[...].astype(F32)
    kv_extra = jnp.concatenate([doc, block], axis=1)
    kv_ref[TOK:PAY, :] = jnp.broadcast_to(kv_extra, (EXTRA, 2 * HD)).astype(BF16)
    outs = [
        pltpu.make_async_copy(kv_ref, kvp_hbm.at[z], out_sems.at[z]) for z in range(ZS)
    ]
    for copy in outs:
        copy.start()
    for copy in copies[4:]:
        copy.wait()
    highs, lows = [], []
    for h in range(GROUP):
        cols = slice(h * HD, (h + 1) * HD)
        prod = qp_ref[0:TOK, WIDE + h * HD : WIDE + (h + 1) * HD].astype(F32) * o_ref[:, cols].astype(F32)
        delta = jnp.sum(prod.T, axis=0, keepdims=True)
        high = delta.astype(BF16).astype(F32)
        highs.append(high)
        lows.append(delta - high)
    zero = jnp.zeros_like(doc)
    first = jnp.concatenate(highs + lows, axis=1)
    second = jnp.concatenate([doc, block] + [zero] * 6, axis=1)
    row = lax.broadcasted_iota(jnp.int32, (EXTRA, 2 * WIDE), 0)
    qp_ref[TOK:PAY, :] = jnp.where(row == 0, first, second).astype(BF16)
    for copy in outs:
        copy.wait()


def code_of(doc, block):
    lane = lax.broadcasted_iota(jnp.int32, doc.shape, 1)
    within = jnp.where(lane < BLK, lane, lane - BLK).astype(F32)
    return doc * TOKENS + block * BLK + within


def score_kernel(n_prev, *refs):
    kv_ref, *rest = refs
    q_refs, rest = rest[:YS], rest[YS:]
    if n_prev:
        place_ref, prev_ref, pt_ref, st_ref, fin_ref, qs, code, bias, keep = rest
    else:
        pt_ref, st_ref, qs, code, bias = rest
    step = pl.program_id(0)

    @pl.when(step == 0)
    def _():
        for x, q_ref in enumerate(q_refs):
            toks = slice(x * TOK, (x + 1) * TOK)
            for h in range(GROUP):
                qs[h, toks, :] = q_ref[0:TOK, h * HD : (h + 1) * HD]
            info = q_ref[TOK:PAY, :].astype(F32)
            doc, block = info[1:2, 0:TOK], info[1:2, TOK : 2 * TOK]
            code[0:1, toks] = code_of(doc, block)
            code[1:2, toks] = doc * TOKENS

    for b in range(2):
        info = kv_ref[b, TOK:PAY, :].astype(F32)
        key_code = code_of(info[0:1, 0:TOK], info[0:1, TOK : 2 * TOK])
        key_code = jnp.broadcast_to(key_code, (TOK, TOK)).T
        for x in range(YS):
            toks = slice(x * TOK, (x + 1) * TOK)
            ok = (key_code <= code[0:1, toks]) & (key_code >= code[1:2, toks])
            bias[b * TOK : (b + 1) * TOK, toks] = jnp.where(ok, 0.0, MASKED)
    keys = jnp.concatenate([kv_ref[0, 0:TOK, 0:HD], kv_ref[1, 0:TOK, 0:HD]], axis=0)
    for h in range(GROUP):
        s = dot(keys, qs[h], NT) + bias[...]
        peak = jnp.maximum(jnp.max(s, axis=0, keepdims=True), FLOOR)
        p = jnp.exp2((s - peak) * EXP2)
        st_ref[0, h : h + 1, :] = peak
        st_ref[0, GROUP + h : GROUP + h + 1, :] = jnp.sum(p, axis=0, keepdims=True)
        pt_ref[:, h * QT : (h + 1) * QT] = p.astype(BF16)
    if n_prev:
        keep[pl.ds(step, 1)] = st_ref[...]

        @pl.when(step == pl.num_programs(0) - 1)
        def _():
            tiles = [prev_ref[t] for t in range(n_prev)] + [keep[t] for t in range(n_prev)]
            top = functools.reduce(jnp.maximum, [t[0:GROUP] for t in tiles])
            total = sum(t[GROUP:] * jnp.exp2((t[0:GROUP] - top) * EXP2) for t in tiles)
            for d in range(YS):
                for x in range(YS):
                    to, of = slice(x * TOK, (x + 1) * TOK), slice((x ^ d) * TOK, ((x ^ d) + 1) * TOK)
                    fin_ref[place_ref[0] ^ d, 0:GROUP, to] = top[:, of]
                    fin_ref[place_ref[0] ^ d, GROUP : 2 * GROUP, to] = total[:, of]


def grad_kernel(last, kv_ref, pt_ref, st_ref, all_ref, *rest):
    q_refs, rest = rest[:YS], rest[YS:]
    if last:
        dq_in, dkv_ref, own_ref, send1, send2, send3, qs, gs, delta, dq = rest
    else:
        dkv_ref, dq, qs, gs, delta = rest
    step = pl.program_id(0)

    @pl.when(step == 0)
    def _():
        for x, q_ref in enumerate(q_refs):
            toks = slice(x * TOK, (x + 1) * TOK)
            info = q_ref[TOK:PAY, :].astype(F32)
            for h in range(GROUP):
                qs[h, toks, :] = q_ref[0:TOK, h * HD : (h + 1) * HD]
                gs[h, toks, :] = q_ref[0:TOK, WIDE + h * HD : WIDE + (h + 1) * HD]
                high = info[0:1, h * TOK : (h + 1) * TOK]
                low = info[0:1, (GROUP + h) * TOK : (GROUP + h + 1) * TOK]
                delta[h : h + 1, toks] = high + low
        dq[...] = dq_in[...] if last else jnp.zeros_like(dq)

    top = functools.reduce(jnp.maximum, [all_ref[y, 0:GROUP] for y in range(YS)])
    total = sum(
        all_ref[y, GROUP : 2 * GROUP] * jnp.exp2((all_ref[y, 0:GROUP] - top) * EXP2)
        for y in range(YS)
    )
    weight = jnp.exp2((st_ref[0, 0:GROUP] - top) * EXP2) / total
    keys = jnp.concatenate([kv_ref[0, 0:TOK, 0:HD], kv_ref[1, 0:TOK, 0:HD]], axis=0)
    values = jnp.concatenate(
        [kv_ref[0, 0:TOK, HD : 2 * HD], kv_ref[1, 0:TOK, HD : 2 * HD]], axis=0
    )
    dk = jnp.zeros((KT, HD), F32)
    dv = jnp.zeros((KT, HD), F32)
    for h in range(GROUP):
        dp = dot(values, gs[h], NT)
        p = pt_ref[:, h * QT : (h + 1) * QT].astype(F32) * weight[h : h + 1]
        ds = (p * (dp - delta[h : h + 1, :])).astype(BF16)
        dv = dv + dot(p.astype(BF16), gs[h])
        dk = dk + dot(ds, qs[h])
        dq[h] += dot(keys, ds, TN)
    dk = dk * SCALE
    for b in range(2):
        rows = slice(b * TOK, (b + 1) * TOK)
        dkv_ref[b, :, 0:HD] = dk[rows].astype(dkv_ref.dtype)
        dkv_ref[b, :, HD : 2 * HD] = dv[rows].astype(dkv_ref.dtype)

    if last:

        @pl.when(step == pl.num_programs(0) - 1)
        def _():
            for x, out in enumerate((own_ref, send1, send2, send3)):
                for h in range(GROUP):
                    part = dq[h, :, x * TOK : (x + 1) * TOK].T * SCALE
                    out[:, h * HD : (h + 1) * HD] = part.astype(out.dtype)


def whole(shape):
    return pl.BlockSpec(shape, lambda *_: (0,) * len(shape))


def shape_of(shape, dtype):
    return jax.ShapeDtypeStruct(shape, dtype)


def params(limit=VMEM_LIMIT):
    return pltpu.CompilerParams(vmem_limit_bytes=limit << 20)


def pack(order, seg, q, k, v, o, g):
    hbm = pl.BlockSpec(memory_space=pltpu.HBM)
    vm = pl.BlockSpec(memory_space=pltpu.VMEM)
    return pl.pallas_call(
        pack_kernel,
        out_shape=(shape_of((ZS, PAY, 2 * HD), BF16), shape_of((PAY, 2 * WIDE), BF16)),
        in_specs=[hbm] * 7,
        out_specs=(hbm, vm),
        scratch_shapes=[
            pltpu.SMEM((2,), jnp.int32),
            pltpu.VMEM((1, TOK), jnp.int32),
            pltpu.VMEM((PAY, 2 * HD), BF16),
            pltpu.VMEM((TOK, GROUP * HD), BF16),
            pltpu.SemaphoreType.DMA((7,)),
            pltpu.SemaphoreType.DMA((ZS,)),
        ],
        compiler_params=params(60),
        name="pack",
    )(order, seg, q, k, v, o, g)


STEPS = ZS // 2
PAIRS = ZS * TOK * GROUP * QT


def scores(kv, queries, prev=None, place=None):
    in_specs = [pl.BlockSpec((2, PAY, 2 * HD), lambda i: (i, 0, 0))]
    in_specs += [whole((PAY, 2 * WIDE))] * YS
    args = [kv, *queries]
    out_shape = [
        shape_of((ZS * TOK, GROUP * QT), BF16),
        shape_of((STEPS, 2 * GROUP, QT), F32),
    ]
    out_specs = [
        pl.BlockSpec((KT, GROUP * QT), lambda i: (i, 0)),
        pl.BlockSpec((1, 2 * GROUP, QT), lambda i: (i, 0, 0)),
    ]
    scratch = [
        pltpu.VMEM((GROUP, QT, HD), BF16),
        pltpu.VMEM((8, QT), F32),
        pltpu.VMEM((KT, QT), F32),
    ]
    if prev is not None:
        in_specs += [pl.BlockSpec(memory_space=pltpu.SMEM), whole(prev.shape)]
        args += [place, prev]
        out_shape.append(shape_of((YS, 2 * GROUP, QT), F32))
        out_specs.append(whole((YS, 2 * GROUP, QT)))
        scratch.append(pltpu.VMEM((STEPS, 2 * GROUP, QT), F32))
    return pl.pallas_call(
        functools.partial(score_kernel, 0 if prev is None else STEPS),
        grid=(STEPS,),
        in_specs=in_specs,
        out_specs=out_specs,
        out_shape=out_shape,
        scratch_shapes=scratch,
        compiler_params=params(),
        cost_estimate=pl.CostEstimate(
            flops=PAIRS, bytes_accessed=1 << 16, transcendentals=0
        ),
        name="scores",
    )(*args)


def grads(kv, probs, stats, all_stats, queries, dq_in=None):
    last = dq_in is not None
    in_specs = [
        pl.BlockSpec((2, PAY, 2 * HD), lambda i: (i, 0, 0)),
        pl.BlockSpec((KT, GROUP * QT), lambda i: (i, 0)),
        pl.BlockSpec((1, 2 * GROUP, QT), lambda i: (i, 0, 0)),
        whole((YS, 2 * GROUP, QT)),
    ] + [whole((PAY, 2 * WIDE))] * YS
    args = [kv, probs, stats, all_stats, *queries]
    dkv_type = F32 if last else BF16
    out_shape = [shape_of((ZS, TOK, 2 * HD), dkv_type)]
    out_specs = [pl.BlockSpec((2, TOK, 2 * HD), lambda i: (i, 0, 0))]
    dq_shape = (GROUP, HD, QT)
    scratch = [
        pltpu.VMEM((GROUP, QT, HD), BF16),
        pltpu.VMEM((GROUP, QT, HD), BF16),
        pltpu.VMEM((8, QT), F32),
    ]
    if last:
        in_specs.append(whole(dq_shape))
        args.append(dq_in)
        out_shape += [shape_of((TOK, GROUP * HD), F32)]
        out_shape += [shape_of((TOK, GROUP * HD), BF16)] * (YS - 1)
        out_specs += [whole((TOK, GROUP * HD))] * YS
        scratch.append(pltpu.VMEM(dq_shape, F32))
    else:
        out_shape.append(shape_of(dq_shape, F32))
        out_specs.append(whole(dq_shape))
    return pl.pallas_call(
        functools.partial(grad_kernel, last),
        grid=(STEPS,),
        in_specs=in_specs,
        out_specs=out_specs,
        out_shape=out_shape,
        scratch_shapes=scratch,
        compiler_params=params(),
        cost_estimate=pl.CostEstimate(
            flops=16 * PAIRS * HD, bytes_accessed=4 << 20, transcendentals=0
        ),
        name="grads",
    )(*args)


def per_device(query, key_rows, value_rows, output, grad_out, block_order, segment):
    n = lax.axis_size("ctx")
    near = [c + 2 * y + 8 * z for z in range(2) for y in range(2) for c in range(2)]
    key_groups = [[r + 4 * y + 16 * z for z in range(4) for y in range(2)] for r in near]
    tile_groups = [
        [c + 4 * y + 16 * z + bits for bits in TILE]
        for z in range(4)
        for y in range(2)
        for c in range(2)
    ]

    def swap(x, bits):
        return lax.ppermute(x, "ctx", [(i, i ^ bits) for i in range(n)])

    def exchange(x, groups):
        return lax.all_to_all(x, "ctx", 0, 0, tiled=True, axis_index_groups=groups)

    kv_pay, q_pay = pack(
        block_order, segment.reshape(1, TOK), query, key_rows, value_rows, output, grad_out
    )
    kv_own = exchange(kv_pay, key_groups)
    queries = [q_pay] + [swap(q_pay, bits) for bits in TILE[1:]]
    kv_own, queries = lax.optimization_barrier((kv_own, queries))
    kv_twin = swap(kv_own, 1)
    p_own, st_own = scores(kv_own, queries)
    index = lax.axis_index("ctx").astype(jnp.int32)
    place = ((index >> 1 & 1) + 2 * (index >> 3 & 1)).reshape(1)
    p_twin, st_twin, stats = scores(kv_twin, queries, st_own, place)
    all_stats = exchange(stats, tile_groups)
    dkv_twin, dq = grads(kv_twin, p_twin, st_twin, all_stats, queries)
    dkv_back = swap(dkv_twin, 1)
    dkv_own, dq_own, *dq_send = grads(kv_own, p_own, st_own, all_stats, queries, dq)
    dkv = (dkv_own + dkv_back.astype(F32)).astype(BF16)
    dkv_all = exchange(dkv, key_groups)
    dq_parts = [swap(part, bits) for part, bits in zip(dq_send, TILE[1:])]
    grad_query = dq_own + sum(part.astype(F32) for part in dq_parts)
    grad_kv = jnp.sum(dkv_all.astype(F32), axis=0).astype(BF16)
    return grad_query.astype(BF16), grad_kv[:, 0:HD], grad_kv[:, HD : 2 * HD]


def solution(mesh):
    both = P("ctx", "kvh")
    return jax.shard_map(
        per_device,
        mesh=mesh,
        in_specs=(both, both, both, both, both, P("ctx"), P("ctx")),
        out_specs=(both, both, both),
        check_vma=False,
    )
```

```python
import functools

import jax
import jax.numpy as jnp
from jax import lax
from jax.experimental import pallas as pl
from jax.experimental.pallas import tpu as pltpu
from jax.sharding import PartitionSpec as P

HEADS = 32
KV_HEADS = 8
HD = 128
GROUP = HEADS // KV_HEADS
BLK = 64
TOKENS = 8192
TOK = 128
EXTRA = 16
PAY = TOK + EXTRA
YS = 4
TILE = (0, 2, 8, 10)
ZS = 8
WIDE = GROUP * HD
QT = YS * TOK
KT = 2 * TOK
SCALE = HD**-0.5
EXP2 = SCALE * 1.4426950408889634
MASKED = -1e30
FLOOR = -1e25
F32 = jnp.float32
BF16 = jnp.bfloat16
VMEM_LIMIT = 24

NT = (((1,), (1,)), ((), ()))
TN = (((0,), (0,)), ((), ()))


def dot(a, b, dims=(((1,), (0,)), ((), ()))):
    return lax.dot_general(a, b, dims, preferred_element_type=F32)


def pack_kernel(
    order_hbm, seg_hbm, q_hbm, k_hbm, v_hbm, o_hbm, g_hbm, kvp_hbm, qp_ref,
    order_ref, seg_ref, kv_ref, o_ref, in_sems, out_sems,
):
    moves = (
        (order_hbm, order_ref),
        (seg_hbm, seg_ref),
        (k_hbm, kv_ref.at[0:TOK, 0:HD]),
        (v_hbm, kv_ref.at[0:TOK, HD : 2 * HD]),
        (q_hbm, qp_ref.at[0:TOK, 0:WIDE]),
        (g_hbm, qp_ref.at[0:TOK, WIDE : 2 * WIDE]),
        (o_hbm, o_ref),
    )
    copies = [
        pltpu.make_async_copy(src, dst, in_sems.at[i]) for i, (src, dst) in enumerate(moves)
    ]
    for copy in copies:
        copy.start()
    for copy in copies[:4]:
        copy.wait()
    lane = lax.broadcasted_iota(jnp.int32, (1, TOK), 1)
    block = jnp.where(lane < BLK, order_ref[0], order_ref[1]).astype(F32)
    doc = seg_ref[...].astype(F32)
    kv_extra = jnp.concatenate([doc, block], axis=1)
    kv_ref[TOK:PAY, :] = jnp.broadcast_to(kv_extra, (EXTRA, 2 * HD)).astype(BF16)
    outs = [
        pltpu.make_async_copy(kv_ref, kvp_hbm.at[z], out_sems.at[z]) for z in range(ZS)
    ]
    for copy in outs:
        copy.start()
    for copy in copies[4:]:
        copy.wait()
    highs, lows = [], []
    for h in range(GROUP):
        cols = slice(h * HD, (h + 1) * HD)
        prod = qp_ref[0:TOK, WIDE + h * HD : WIDE + (h + 1) * HD].astype(F32) * o_ref[:, cols].astype(F32)
        delta = jnp.sum(prod.T, axis=0, keepdims=True)
        high = delta.astype(BF16).astype(F32)
        highs.append(high)
        lows.append(delta - high)
    zero = jnp.zeros_like(doc)
    first = jnp.concatenate(highs + lows, axis=1)
    second = jnp.concatenate([doc, block] + [zero] * 6, axis=1)
    row = lax.broadcasted_iota(jnp.int32, (EXTRA, 2 * WIDE), 0)
    qp_ref[TOK:PAY, :] = jnp.where(row == 0, first, second).astype(BF16)
    for copy in outs:
        copy.wait()


def code_of(doc, block):
    lane = lax.broadcasted_iota(jnp.int32, doc.shape, 1)
    within = jnp.where(lane < BLK, lane, lane - BLK).astype(F32)
    return doc * TOKENS + block * BLK + within


def score_kernel(n_q, last, kv_ref, *refs):
    q_refs, refs = refs[:n_q], refs[n_q:]
    if last:
        place_ref, near_ref, far_ref, pt_ref, st_ref, fin_ref, qs, code, bias = refs
    else:
        pt_ref, st_ref, qs, code, bias = refs
    width = n_q * TOK
    for x, q_ref in enumerate(q_refs):
        toks = slice(x * TOK, (x + 1) * TOK)
        for h in range(GROUP):
            qs[h, toks, :] = q_ref[0:TOK, h * HD : (h + 1) * HD]
        info = q_ref[TOK:PAY, :].astype(F32)
        doc, block = info[1:2, 0:TOK], info[1:2, TOK : 2 * TOK]
        code[0:1, toks] = code_of(doc, block)
        code[1:2, toks] = doc * TOKENS

    for step in range(STEPS):
        for b in range(2):
            info = kv_ref[2 * step + b, TOK:PAY, :].astype(F32)
            key_code = code_of(info[0:1, 0:TOK], info[0:1, TOK : 2 * TOK])
            key_code = jnp.broadcast_to(key_code, (TOK, TOK)).T
            for x in range(n_q):
                toks = slice(x * TOK, (x + 1) * TOK)
                ok = (key_code <= code[0:1, toks]) & (key_code >= code[1:2, toks])
                bias[step % 2, b * TOK : (b + 1) * TOK, toks] = jnp.where(ok, 0.0, MASKED)
        rows = slice(step * KT, (step + 1) * KT)
        keys = jnp.concatenate([kv_ref[2 * step + b, 0:TOK, 0:HD] for b in range(2)], axis=0)
        for h in range(GROUP):
            s = dot(keys, qs[h], NT) + bias[step % 2]
            peak = jnp.maximum(jnp.max(s, axis=0, keepdims=True), FLOOR)
            p = jnp.exp2((s - peak) * EXP2)
            st_ref[step, h : h + 1, :] = peak
            st_ref[step, GROUP + h : GROUP + h + 1, :] = jnp.sum(p, axis=0, keepdims=True)
            pt_ref[rows, h * width : (h + 1) * width] = p.astype(BF16)
    if last:
        tiles = [jnp.concatenate([near_ref[t], far_ref[t]], axis=1) for t in range(STEPS)]
        tiles += [st_ref[t] for t in range(STEPS)]
        top = functools.reduce(jnp.maximum, [t[0:GROUP] for t in tiles])
        total = sum(t[GROUP:] * jnp.exp2((t[0:GROUP] - top) * EXP2) for t in tiles)
        for d in range(YS):
            for x in range(YS):
                to, of = slice(x * TOK, (x + 1) * TOK), slice((x ^ d) * TOK, ((x ^ d) + 1) * TOK)
                fin_ref[place_ref[0] ^ d, 0:GROUP, to] = top[:, of]
                fin_ref[place_ref[0] ^ d, GROUP : 2 * GROUP, to] = total[:, of]


def grad_kernel(last, n_parts, kv_ref, all_ref, *refs):
    p_refs, refs = refs[:n_parts], refs[n_parts:]
    st_refs, refs = refs[:n_parts], refs[n_parts:]
    q_refs, refs = refs[:YS], refs[YS:]
    if last:
        dq_in, dkv_ref, own_ref, send1, send2, send3, qs, gs, delta, dq = refs
    else:
        dkv_ref, dq, qs, gs, delta = refs
    for x, q_ref in enumerate(q_refs):
        toks = slice(x * TOK, (x + 1) * TOK)
        info = q_ref[TOK:PAY, :].astype(F32)
        for h in range(GROUP):
            qs[h, toks, :] = q_ref[0:TOK, h * HD : (h + 1) * HD]
            gs[h, toks, :] = q_ref[0:TOK, WIDE + h * HD : WIDE + (h + 1) * HD]
            high = info[0:1, h * TOK : (h + 1) * TOK]
            low = info[0:1, (GROUP + h) * TOK : (GROUP + h + 1) * TOK]
            delta[h : h + 1, toks] = high + low
    dq[...] = dq_in[...] if last else jnp.zeros_like(dq)
    width = QT // n_parts

    top = functools.reduce(jnp.maximum, [all_ref[y, 0:GROUP] for y in range(YS)])
    total = sum(
        all_ref[y, GROUP : 2 * GROUP] * jnp.exp2((all_ref[y, 0:GROUP] - top) * EXP2)
        for y in range(YS)
    )
    for step in range(STEPS):
        rows = slice(step * KT, (step + 1) * KT)
        peaks = jnp.concatenate([st_ref[step, 0:GROUP] for st_ref in st_refs], axis=1)
        weight = jnp.exp2((peaks - top) * EXP2) / total
        pair = [kv_ref[2 * step + b, 0:TOK] for b in range(2)]
        keys = jnp.concatenate([part[:, 0:HD] for part in pair], axis=0)
        values = jnp.concatenate([part[:, HD : 2 * HD] for part in pair], axis=0)
        dk = jnp.zeros((KT, HD), F32)
        dv = jnp.zeros((KT, HD), F32)
        for h in range(GROUP):
            cols = slice(h * width, (h + 1) * width)
            dp = dot(values, gs[h], NT)
            p = jnp.concatenate([p_ref[rows, cols] for p_ref in p_refs], axis=1)
            p = p.astype(F32) * weight[h : h + 1]
            ds = (p * (dp - delta[h : h + 1, :])).astype(BF16)
            dv = dv + dot(p.astype(BF16), gs[h])
            dk = dk + dot(ds, qs[h])
            dq[h] += dot(keys, ds, TN)
        dk = dk * SCALE
        for b in range(2):
            half = slice(b * TOK, (b + 1) * TOK)
            dkv_ref[2 * step + b, :, 0:HD] = dk[half].astype(dkv_ref.dtype)
            dkv_ref[2 * step + b, :, HD : 2 * HD] = dv[half].astype(dkv_ref.dtype)

    if last:
        for x, out in enumerate((own_ref, send1, send2, send3)):
            for h in range(GROUP):
                part = dq[h, :, x * TOK : (x + 1) * TOK].T * SCALE
                out[:, h * HD : (h + 1) * HD] = part.astype(out.dtype)


def shape_of(shape, dtype):
    return jax.ShapeDtypeStruct(shape, dtype)


def params(limit=VMEM_LIMIT):
    return pltpu.CompilerParams(vmem_limit_bytes=limit << 20)


def pack(order, seg, q, k, v, o, g):
    hbm = pl.BlockSpec(memory_space=pltpu.HBM)
    vm = pl.BlockSpec(memory_space=pltpu.VMEM)
    return pl.pallas_call(
        pack_kernel,
        out_shape=(shape_of((ZS, PAY, 2 * HD), BF16), shape_of((PAY, 2 * WIDE), BF16)),
        in_specs=[hbm] * 7,
        out_specs=(hbm, vm),
        scratch_shapes=[
            pltpu.SMEM((2,), jnp.int32),
            pltpu.VMEM((1, TOK), jnp.int32),
            pltpu.VMEM((PAY, 2 * HD), BF16),
            pltpu.VMEM((TOK, GROUP * HD), BF16),
            pltpu.SemaphoreType.DMA((7,)),
            pltpu.SemaphoreType.DMA((ZS,)),
        ],
        compiler_params=params(60),
        name="pack",
    )(order, seg, q, k, v, o, g)


STEPS = ZS // 2
VMEM = pl.BlockSpec(memory_space=pltpu.VMEM)
SMEM = pl.BlockSpec(memory_space=pltpu.SMEM)
STATS = (2 * GROUP, QT)
STATED = {"near": 10**8, "far": 46 * 10**8, "twin": 46 * 10**8, "grads": 6 * 10**9}


def cost(kind):
    return pl.CostEstimate(flops=STATED[kind], bytes_accessed=1 << 16, transcendentals=0)


def scores(kind, kv, queries, prev=None, place=None):
    width = len(queries) * TOK
    args = [kv, *queries]
    in_specs = [VMEM] * len(args)
    out_shape = [
        shape_of((ZS * TOK, GROUP * width), BF16),
        shape_of((STEPS, 2 * GROUP, width), F32),
    ]
    if prev is not None:
        args += [place, *prev]
        in_specs += [SMEM, VMEM, VMEM]
        out_shape.append(shape_of((YS, *STATS), F32))
    return pl.pallas_call(
        functools.partial(score_kernel, len(queries), prev is not None),
        in_specs=in_specs,
        out_specs=[VMEM] * len(out_shape),
        out_shape=out_shape,
        scratch_shapes=[
            pltpu.VMEM((GROUP, width, HD), BF16),
            pltpu.VMEM((8, width), F32),
            pltpu.VMEM((2, KT, width), F32),
        ],
        compiler_params=params(),
        cost_estimate=cost(kind),
        name="scores_" + kind,
    )(*args)


def grads(kv, probs, stats, all_stats, queries, dq_in=None):
    last = dq_in is not None
    dq_shape = (GROUP, HD, QT)
    args = [kv, all_stats, *probs, *stats, *queries]
    out_shape = [shape_of((ZS, TOK, 2 * HD), F32 if last else BF16)]
    scratch = [
        pltpu.VMEM((GROUP, QT, HD), BF16),
        pltpu.VMEM((GROUP, QT, HD), BF16),
        pltpu.VMEM((8, QT), F32),
    ]
    if last:
        args.append(dq_in)
        out_shape += [shape_of((TOK, WIDE), F32)] + [shape_of((TOK, WIDE), BF16)] * (YS - 1)
        scratch.append(pltpu.VMEM(dq_shape, F32))
    else:
        out_shape.append(shape_of(dq_shape, F32))
    return pl.pallas_call(
        functools.partial(grad_kernel, last, len(probs)),
        in_specs=[VMEM] * len(args),
        out_specs=[VMEM] * len(out_shape),
        out_shape=out_shape,
        scratch_shapes=scratch,
        compiler_params=params(),
        cost_estimate=cost("grads"),
        name="grads",
    )(*args)


def per_device(query, key_rows, value_rows, output, grad_out, block_order, segment):
    n = lax.axis_size("ctx")
    near = [c + 2 * y + 8 * z for z in range(2) for y in range(2) for c in range(2)]
    key_groups = [[r + 4 * y + 16 * z for z in range(4) for y in range(2)] for r in near]
    tile_groups = [
        [c + 4 * y + 16 * z + bits for bits in TILE]
        for z in range(4)
        for y in range(2)
        for c in range(2)
    ]

    def swap(x, bits):
        return lax.ppermute(x, "ctx", [(i, i ^ bits) for i in range(n)])

    def exchange(x, groups):
        return lax.all_to_all(x, "ctx", 0, 0, tiled=True, axis_index_groups=groups)

    kv_pay, q_pay = pack(
        block_order, segment.reshape(1, TOK), query, key_rows, value_rows, output, grad_out
    )
    kv_own = exchange(kv_pay, key_groups)
    queries = [q_pay] + [swap(q_pay, bits) for bits in TILE[1:]]
    kv_twin = swap(kv_own, 1)
    index = lax.axis_index("ctx").astype(jnp.int32)
    place = ((index >> 1 & 1) + 2 * (index >> 3 & 1)).reshape(1)
    p_near, st_near = scores("near", kv_own, queries[:2])
    st_near, far = lax.optimization_barrier((st_near, queries[2:]))
    queries = queries[:2] + far
    p_far, st_far = scores("far", kv_own, far)
    p_twin, st_twin, stats = scores("twin", kv_twin, queries, (st_near, st_far), place)
    all_stats = exchange(stats, tile_groups)
    dkv_twin, dq = grads(kv_twin, [p_twin], [st_twin], all_stats, queries)
    dkv_back = swap(dkv_twin, 1)
    dkv_own, dq_own, *dq_send = grads(
        kv_own, [p_near, p_far], [st_near, st_far], all_stats, queries, dq
    )
    dkv = (dkv_own + dkv_back.astype(F32)).astype(BF16)
    dkv_all = exchange(dkv, key_groups)
    dq_parts = [swap(part, bits) for part, bits in zip(dq_send, TILE[1:])]
    grad_query = dq_own + sum(part.astype(F32) for part in dq_parts)
    grad_kv = jnp.sum(dkv_all.astype(F32), axis=0).astype(BF16)
    return grad_query.astype(BF16), grad_kv[:, 0:HD], grad_kv[:, HD : 2 * HD]


def solution(mesh):
    both = P("ctx", "kvh")
    return jax.shard_map(
        per_device,
        mesh=mesh,
        in_specs=(both, both, both, both, both, P("ctx"), P("ctx")),
        out_specs=(both, both, both),
        check_vma=False,
    )
```

```python
import functools

import jax
import jax.numpy as jnp
from jax import lax
from jax.experimental import pallas as pl
from jax.experimental.pallas import tpu as pltpu
from jax.sharding import PartitionSpec as P

HEADS = 32
KV_HEADS = 8
HD = 128
GROUP = HEADS // KV_HEADS
BLK = 64
TOKENS = 8192
TOK = 128
EXTRA = 16
PAY = TOK + EXTRA
YS = 4
TILE = (0, 2, 4, 6)
ZS = 8
WIDE = GROUP * HD
QT = YS * TOK
KT = 2 * TOK
SCALE = HD**-0.5
EXP2 = SCALE * 1.4426950408889634
MASKED = -1e30
FLOOR = -1e25
F32 = jnp.float32
BF16 = jnp.bfloat16
VMEM_LIMIT = 24

NT = (((1,), (1,)), ((), ()))
TN = (((0,), (0,)), ((), ()))


def dot(a, b, dims=(((1,), (0,)), ((), ()))):
    return lax.dot_general(a, b, dims, preferred_element_type=F32)


def pack_kernel(
    order_hbm, seg_hbm, q_hbm, k_hbm, v_hbm, o_hbm, g_hbm, kvp_hbm, qp_ref,
    order_ref, seg_ref, kv_ref, o_ref, in_sems, out_sems,
):
    moves = (
        (order_hbm, order_ref),
        (seg_hbm, seg_ref),
        (k_hbm, kv_ref.at[0:TOK, 0:HD]),
        (v_hbm, kv_ref.at[0:TOK, HD : 2 * HD]),
        (q_hbm, qp_ref.at[0:TOK, 0:WIDE]),
        (g_hbm, qp_ref.at[0:TOK, WIDE : 2 * WIDE]),
        (o_hbm, o_ref),
    )
    copies = [
        pltpu.make_async_copy(src, dst, in_sems.at[i]) for i, (src, dst) in enumerate(moves)
    ]
    for copy in copies:
        copy.start()
    for copy in copies[:4]:
        copy.wait()
    lane = lax.broadcasted_iota(jnp.int32, (1, TOK), 1)
    block = jnp.where(lane < BLK, order_ref[0], order_ref[1]).astype(F32)
    doc = seg_ref[...].astype(F32)
    kv_extra = jnp.concatenate([doc, block], axis=1)
    kv_ref[TOK:PAY, :] = jnp.broadcast_to(kv_extra, (EXTRA, 2 * HD)).astype(BF16)
    outs = [
        pltpu.make_async_copy(kv_ref, kvp_hbm.at[z], out_sems.at[z]) for z in range(ZS)
    ]
    for copy in outs:
        copy.start()
    for copy in copies[4:]:
        copy.wait()
    highs, lows = [], []
    for h in range(GROUP):
        cols = slice(h * HD, (h + 1) * HD)
        prod = qp_ref[0:TOK, WIDE + h * HD : WIDE + (h + 1) * HD].astype(F32) * o_ref[:, cols].astype(F32)
        delta = jnp.sum(prod.T, axis=0, keepdims=True)
        high = delta.astype(BF16).astype(F32)
        highs.append(high)
        lows.append(delta - high)
    zero = jnp.zeros_like(doc)
    first = jnp.concatenate(highs + lows, axis=1)
    second = jnp.concatenate([doc, block] + [zero] * 6, axis=1)
    row = lax.broadcasted_iota(jnp.int32, (EXTRA, 2 * WIDE), 0)
    qp_ref[TOK:PAY, :] = jnp.where(row == 0, first, second).astype(BF16)
    for copy in outs:
        copy.wait()


def code_of(doc, block):
    lane = lax.broadcasted_iota(jnp.int32, doc.shape, 1)
    within = jnp.where(lane < BLK, lane, lane - BLK).astype(F32)
    return doc * TOKENS + block * BLK + within


def score_kernel(n_q, last, kv_ref, *refs):
    q_refs, refs = refs[:n_q], refs[n_q:]
    if last:
        place_ref, near_ref, far_ref, pt_ref, st_ref, fin_ref, qs, code, bias = refs
    else:
        pt_ref, st_ref, qs, code, bias = refs
    width = n_q * TOK
    for x, q_ref in enumerate(q_refs):
        toks = slice(x * TOK, (x + 1) * TOK)
        for h in range(GROUP):
            qs[h, toks, :] = q_ref[0:TOK, h * HD : (h + 1) * HD]
        info = q_ref[TOK:PAY, :].astype(F32)
        doc, block = info[1:2, 0:TOK], info[1:2, TOK : 2 * TOK]
        code[0:1, toks] = code_of(doc, block)
        code[1:2, toks] = doc * TOKENS

    for step in range(STEPS):
        for b in range(2):
            info = kv_ref[2 * step + b, TOK:PAY, :].astype(F32)
            key_code = code_of(info[0:1, 0:TOK], info[0:1, TOK : 2 * TOK])
            key_code = jnp.broadcast_to(key_code, (TOK, TOK)).T
            for x in range(n_q):
                toks = slice(x * TOK, (x + 1) * TOK)
                ok = (key_code <= code[0:1, toks]) & (key_code >= code[1:2, toks])
                bias[step % 2, b * TOK : (b + 1) * TOK, toks] = jnp.where(ok, 0.0, MASKED)
        rows = slice(step * KT, (step + 1) * KT)
        keys = jnp.concatenate([kv_ref[2 * step + b, 0:TOK, 0:HD] for b in range(2)], axis=0)
        for h in range(GROUP):
            s = dot(keys, qs[h], NT) + bias[step % 2]
            peak = jnp.maximum(jnp.max(s, axis=0, keepdims=True), FLOOR)
            p = jnp.exp2((s - peak) * EXP2)
            st_ref[step, h : h + 1, :] = peak
            st_ref[step, GROUP + h : GROUP + h + 1, :] = jnp.sum(p, axis=0, keepdims=True)
            pt_ref[rows, h * width : (h + 1) * width] = p.astype(BF16)
    if last:
        tiles = [jnp.concatenate([near_ref[t], far_ref[t]], axis=1) for t in range(STEPS)]
        tiles += [st_ref[t] for t in range(STEPS)]
        top = functools.reduce(jnp.maximum, [t[0:GROUP] for t in tiles])
        total = sum(t[GROUP:] * jnp.exp2((t[0:GROUP] - top) * EXP2) for t in tiles)
        for d in range(YS):
            for x in range(YS):
                to, of = slice(x * TOK, (x + 1) * TOK), slice((x ^ d) * TOK, ((x ^ d) + 1) * TOK)
                fin_ref[place_ref[0] ^ d, 0:GROUP, to] = top[:, of]
                fin_ref[place_ref[0] ^ d, GROUP : 2 * GROUP, to] = total[:, of]


def grad_kernel(last, n_parts, kv_ref, all_ref, *refs):
    p_refs, refs = refs[:n_parts], refs[n_parts:]
    st_refs, refs = refs[:n_parts], refs[n_parts:]
    q_refs, refs = refs[:YS], refs[YS:]
    if last:
        dq_in, dkv_ref, own_ref, send1, send2, send3, qs, gs, delta, dq = refs
    else:
        dkv_ref, dq, qs, gs, delta = refs
    for x, q_ref in enumerate(q_refs):
        toks = slice(x * TOK, (x + 1) * TOK)
        info = q_ref[TOK:PAY, :].astype(F32)
        for h in range(GROUP):
            qs[h, toks, :] = q_ref[0:TOK, h * HD : (h + 1) * HD]
            gs[h, toks, :] = q_ref[0:TOK, WIDE + h * HD : WIDE + (h + 1) * HD]
            high = info[0:1, h * TOK : (h + 1) * TOK]
            low = info[0:1, (GROUP + h) * TOK : (GROUP + h + 1) * TOK]
            delta[h : h + 1, toks] = high + low
    dq[...] = dq_in[...] if last else jnp.zeros_like(dq)
    width = QT // n_parts

    top = functools.reduce(jnp.maximum, [all_ref[y, 0:GROUP] for y in range(YS)])
    total = sum(
        all_ref[y, GROUP : 2 * GROUP] * jnp.exp2((all_ref[y, 0:GROUP] - top) * EXP2)
        for y in range(YS)
    )
    for step in range(STEPS):
        rows = slice(step * KT, (step + 1) * KT)
        peaks = jnp.concatenate([st_ref[step, 0:GROUP] for st_ref in st_refs], axis=1)
        weight = jnp.exp2((peaks - top) * EXP2) / total
        pair = [kv_ref[2 * step + b, 0:TOK] for b in range(2)]
        keys = jnp.concatenate([part[:, 0:HD] for part in pair], axis=0)
        values = jnp.concatenate([part[:, HD : 2 * HD] for part in pair], axis=0)
        dk = jnp.zeros((KT, HD), F32)
        dv = jnp.zeros((KT, HD), F32)
        for h in range(GROUP):
            cols = slice(h * width, (h + 1) * width)
            dp = dot(values, gs[h], NT)
            p = jnp.concatenate([p_ref[rows, cols] for p_ref in p_refs], axis=1)
            p = p.astype(F32) * weight[h : h + 1]
            ds = (p * (dp - delta[h : h + 1, :])).astype(BF16)
            dv = dv + dot(p.astype(BF16), gs[h])
            dk = dk + dot(ds, qs[h])
            dq[h] += dot(keys, ds, TN)
        dk = dk * SCALE
        for b in range(2):
            half = slice(b * TOK, (b + 1) * TOK)
            dkv_ref[2 * step + b, :, 0:HD] = dk[half].astype(dkv_ref.dtype)
            dkv_ref[2 * step + b, :, HD : 2 * HD] = dv[half].astype(dkv_ref.dtype)

    if last:
        for x, out in enumerate((own_ref, send1, send2, send3)):
            for h in range(GROUP):
                part = dq[h, :, x * TOK : (x + 1) * TOK].T * SCALE
                out[:, h * HD : (h + 1) * HD] = part.astype(out.dtype)


def shape_of(shape, dtype):
    return jax.ShapeDtypeStruct(shape, dtype)


def params(limit=VMEM_LIMIT):
    return pltpu.CompilerParams(vmem_limit_bytes=limit << 20)


def pack(order, seg, q, k, v, o, g):
    hbm = pl.BlockSpec(memory_space=pltpu.HBM)
    vm = pl.BlockSpec(memory_space=pltpu.VMEM)
    return pl.pallas_call(
        pack_kernel,
        out_shape=(shape_of((ZS, PAY, 2 * HD), BF16), shape_of((PAY, 2 * WIDE), BF16)),
        in_specs=[hbm] * 7,
        out_specs=(hbm, vm),
        scratch_shapes=[
            pltpu.SMEM((2,), jnp.int32),
            pltpu.VMEM((1, TOK), jnp.int32),
            pltpu.VMEM((PAY, 2 * HD), BF16),
            pltpu.VMEM((TOK, GROUP * HD), BF16),
            pltpu.SemaphoreType.DMA((7,)),
            pltpu.SemaphoreType.DMA((ZS,)),
        ],
        compiler_params=params(60),
        name="pack",
    )(order, seg, q, k, v, o, g)


STEPS = ZS // 2
VMEM = pl.BlockSpec(memory_space=pltpu.VMEM)
SMEM = pl.BlockSpec(memory_space=pltpu.SMEM)
STATS = (2 * GROUP, QT)
STATED = {"near": 10**8, "far": 46 * 10**8, "twin": 46 * 10**8, "grads": 6 * 10**9}


def cost(kind):
    return pl.CostEstimate(flops=STATED[kind], bytes_accessed=1 << 16, transcendentals=0)


def scores(kind, kv, queries, prev=None, place=None):
    width = len(queries) * TOK
    args = [kv, *queries]
    in_specs = [VMEM] * len(args)
    out_shape = [
        shape_of((ZS * TOK, GROUP * width), BF16),
        shape_of((STEPS, 2 * GROUP, width), F32),
    ]
    if prev is not None:
        args += [place, *prev]
        in_specs += [SMEM, VMEM, VMEM]
        out_shape.append(shape_of((YS, *STATS), F32))
    return pl.pallas_call(
        functools.partial(score_kernel, len(queries), prev is not None),
        in_specs=in_specs,
        out_specs=[VMEM] * len(out_shape),
        out_shape=out_shape,
        scratch_shapes=[
            pltpu.VMEM((GROUP, width, HD), BF16),
            pltpu.VMEM((8, width), F32),
            pltpu.VMEM((2, KT, width), F32),
        ],
        compiler_params=params(),
        cost_estimate=cost(kind),
        name="scores_" + kind,
    )(*args)


def grads(kv, probs, stats, all_stats, queries, dq_in=None):
    last = dq_in is not None
    dq_shape = (GROUP, HD, QT)
    args = [kv, all_stats, *probs, *stats, *queries]
    out_shape = [shape_of((ZS, TOK, 2 * HD), F32 if last else BF16)]
    scratch = [
        pltpu.VMEM((GROUP, QT, HD), BF16),
        pltpu.VMEM((GROUP, QT, HD), BF16),
        pltpu.VMEM((8, QT), F32),
    ]
    if last:
        args.append(dq_in)
        out_shape += [shape_of((TOK, WIDE), F32)] + [shape_of((TOK, WIDE), BF16)] * (YS - 1)
        scratch.append(pltpu.VMEM(dq_shape, F32))
    else:
        out_shape.append(shape_of(dq_shape, F32))
    return pl.pallas_call(
        functools.partial(grad_kernel, last, len(probs)),
        in_specs=[VMEM] * len(args),
        out_specs=[VMEM] * len(out_shape),
        out_shape=out_shape,
        scratch_shapes=scratch,
        compiler_params=params(),
        cost_estimate=cost("grads"),
        name="grads",
    )(*args)


def per_device(query, key_rows, value_rows, output, grad_out, block_order, segment):
    n = lax.axis_size("ctx")
    key_groups = [[r + 8 * z for z in range(ZS)] for r in range(ZS)]
    tile_groups = [[c + 8 * z + bits for bits in TILE] for z in range(ZS) for c in range(2)]

    def swap(x, bits):
        return lax.ppermute(x, "ctx", [(i, i ^ bits) for i in range(n)])

    def exchange(x, groups):
        return lax.all_to_all(x, "ctx", 0, 0, tiled=True, axis_index_groups=groups)

    kv_pay, q_pay = pack(
        block_order, segment.reshape(1, TOK), query, key_rows, value_rows, output, grad_out
    )
    kv_own = exchange(kv_pay, key_groups)
    q_far, q_near = swap(q_pay, TILE[2]), swap(q_pay, TILE[1])
    queries = [q_pay, q_near, q_far, swap(q_far, TILE[1])]
    kv_twin = swap(kv_own, 1)
    index = lax.axis_index("ctx").astype(jnp.int32)
    place = (index >> 1 & (YS - 1)).reshape(1)
    p_near, st_near = scores("near", kv_own, queries[:2])
    st_near, far = lax.optimization_barrier((st_near, queries[2:]))
    queries = queries[:2] + far
    p_far, st_far = scores("far", kv_own, far)
    p_twin, st_twin, stats = scores("twin", kv_twin, queries, (st_near, st_far), place)
    all_stats = exchange(stats, tile_groups)
    dkv_twin, dq = grads(kv_twin, [p_twin], [st_twin], all_stats, queries)
    dkv_back = swap(dkv_twin, 1)
    dkv_own, dq_own, *dq_send = grads(
        kv_own, [p_near, p_far], [st_near, st_far], all_stats, queries, dq
    )
    dkv = (dkv_own + dkv_back.astype(F32)).astype(BF16)
    dkv_all = exchange(dkv, key_groups)
    dq_parts = [swap(part, bits) for part, bits in zip(dq_send[::-1], TILE[:0:-1])]
    grad_query = dq_own + sum(part.astype(F32) for part in dq_parts)
    grad_kv = jnp.sum(dkv_all.astype(F32), axis=0).astype(BF16)
    return grad_query.astype(BF16), grad_kv[:, 0:HD], grad_kv[:, HD : 2 * HD]


def solution(mesh):
    both = P("ctx", "kvh")
    return jax.shard_map(
        per_device,
        mesh=mesh,
        in_specs=(both, both, both, both, both, P("ctx"), P("ctx")),
        out_specs=(both, both, both),
        check_vma=False,
    )
```

```python
import functools

import jax
import jax.numpy as jnp
from jax import lax
from jax.experimental import pallas as pl
from jax.experimental.pallas import tpu as pltpu
from jax.sharding import PartitionSpec as P

HEADS = 32
KV_HEADS = 8
HD = 128
GROUP = HEADS // KV_HEADS
BLK = 64
TOKENS = 8192
TOK = 128
EXTRA = 16
PAY = TOK + EXTRA
YS = 4
TILE = (0, 2, 4, 6)
ZS = 8
WIDE = GROUP * HD
QT = YS * TOK
KT = 2 * TOK
SCALE = HD**-0.5
EXP2 = SCALE * 1.4426950408889634
MASKED = -1e30
FLOOR = -1e25
F32 = jnp.float32
BF16 = jnp.bfloat16
VMEM_LIMIT = 24

NT = (((1,), (1,)), ((), ()))
TN = (((0,), (0,)), ((), ()))


def dot(a, b, dims=(((1,), (0,)), ((), ()))):
    return lax.dot_general(a, b, dims, preferred_element_type=F32)


def pack_kernel(
    order_hbm, seg_hbm, q_hbm, k_hbm, v_hbm, o_hbm, g_hbm, kvp_hbm, qp_ref,
    order_ref, seg_ref, kv_ref, o_ref, in_sems, out_sems,
):
    moves = (
        (order_hbm, order_ref),
        (seg_hbm, seg_ref),
        (k_hbm, kv_ref.at[0:TOK, 0:HD]),
        (v_hbm, kv_ref.at[0:TOK, HD : 2 * HD]),
        (q_hbm, qp_ref.at[0:TOK, 0:WIDE]),
        (g_hbm, qp_ref.at[0:TOK, WIDE : 2 * WIDE]),
        (o_hbm, o_ref),
    )
    copies = [
        pltpu.make_async_copy(src, dst, in_sems.at[i]) for i, (src, dst) in enumerate(moves)
    ]
    for copy in copies:
        copy.start()
    for copy in copies[:4]:
        copy.wait()
    lane = lax.broadcasted_iota(jnp.int32, (1, TOK), 1)
    block = jnp.where(lane < BLK, order_ref[0], order_ref[1]).astype(F32)
    doc = seg_ref[...].astype(F32)
    kv_extra = jnp.concatenate([doc, block], axis=1)
    kv_ref[TOK:PAY, :] = jnp.broadcast_to(kv_extra, (EXTRA, 2 * HD)).astype(BF16)
    outs = [
        pltpu.make_async_copy(kv_ref, kvp_hbm.at[z], out_sems.at[z]) for z in range(ZS)
    ]
    for copy in outs:
        copy.start()
    for copy in copies[4:]:
        copy.wait()
    highs, lows = [], []
    for h in range(GROUP):
        cols = slice(h * HD, (h + 1) * HD)
        prod = qp_ref[0:TOK, WIDE + h * HD : WIDE + (h + 1) * HD].astype(F32) * o_ref[:, cols].astype(F32)
        delta = jnp.sum(prod.T, axis=0, keepdims=True)
        high = delta.astype(BF16).astype(F32)
        highs.append(high)
        lows.append(delta - high)
    zero = jnp.zeros_like(doc)
    first = jnp.concatenate(highs + lows, axis=1)
    second = jnp.concatenate([doc, block] + [zero] * 6, axis=1)
    row = lax.broadcasted_iota(jnp.int32, (EXTRA, 2 * WIDE), 0)
    qp_ref[TOK:PAY, :] = jnp.where(row == 0, first, second).astype(BF16)
    for copy in outs:
        copy.wait()


def code_of(doc, block):
    lane = lax.broadcasted_iota(jnp.int32, doc.shape, 1)
    within = jnp.where(lane < BLK, lane, lane - BLK).astype(F32)
    return doc * TOKENS + block * BLK + within


def score_kernel(n_q, last, kv_ref, *refs):
    q_refs, refs = refs[:n_q], refs[n_q:]
    if last:
        place_ref, near_own, near_twin, far_own, pt_ref, st_ref, fin_ref, qs, code, bias = refs
    else:
        pt_ref, st_ref, qs, code, bias = refs
    width = n_q * TOK
    for x, q_ref in enumerate(q_refs):
        toks = slice(x * TOK, (x + 1) * TOK)
        for h in range(GROUP):
            qs[h, toks, :] = q_ref[0:TOK, h * HD : (h + 1) * HD]
        info = q_ref[TOK:PAY, :].astype(F32)
        doc, block = info[1:2, 0:TOK], info[1:2, TOK : 2 * TOK]
        code[0:1, toks] = code_of(doc, block)
        code[1:2, toks] = doc * TOKENS

    for step in range(STEPS):
        for b in range(2):
            info = kv_ref[2 * step + b, TOK:PAY, :].astype(F32)
            key_code = code_of(info[0:1, 0:TOK], info[0:1, TOK : 2 * TOK])
            key_code = jnp.broadcast_to(key_code, (TOK, TOK)).T
            for x in range(n_q):
                toks = slice(x * TOK, (x + 1) * TOK)
                ok = (key_code <= code[0:1, toks]) & (key_code >= code[1:2, toks])
                bias[step % 2, b * TOK : (b + 1) * TOK, toks] = jnp.where(ok, 0.0, MASKED)
        rows = slice(step * KT, (step + 1) * KT)
        keys = jnp.concatenate([kv_ref[2 * step + b, 0:TOK, 0:HD] for b in range(2)], axis=0)
        for h in range(GROUP):
            s = dot(keys, qs[h], NT) + bias[step % 2]
            peak = jnp.maximum(jnp.max(s, axis=0, keepdims=True), FLOOR)
            p = jnp.exp2((s - peak) * EXP2)
            st_ref[step, h : h + 1, :] = peak
            st_ref[step, GROUP + h : GROUP + h + 1, :] = jnp.sum(p, axis=0, keepdims=True)
            pt_ref[rows, h * width : (h + 1) * width] = p.astype(BF16)
    if last:
        tiles = [
            jnp.concatenate([near_ref[t], far_ref[t]], axis=1)
            for near_ref, far_ref in ((near_own, far_own), (near_twin, st_ref))
            for t in range(STEPS)
        ]
        top = functools.reduce(jnp.maximum, [t[0:GROUP] for t in tiles])
        total = sum(t[GROUP:] * jnp.exp2((t[0:GROUP] - top) * EXP2) for t in tiles)
        for d in range(YS):
            for x in range(YS):
                to, of = slice(x * TOK, (x + 1) * TOK), slice((x ^ d) * TOK, ((x ^ d) + 1) * TOK)
                fin_ref[place_ref[0] ^ d, 0:GROUP, to] = top[:, of]
                fin_ref[place_ref[0] ^ d, GROUP : 2 * GROUP, to] = total[:, of]


def grad_kernel(last, n_parts, kv_ref, all_ref, *refs):
    p_refs, refs = refs[:n_parts], refs[n_parts:]
    st_refs, refs = refs[:n_parts], refs[n_parts:]
    q_refs, refs = refs[:YS], refs[YS:]
    if last:
        dq_in, dkv_ref, own_ref, send1, send2, send3, qs, gs, delta, dq = refs
    else:
        dkv_ref, dq, qs, gs, delta = refs
    for x, q_ref in enumerate(q_refs):
        toks = slice(x * TOK, (x + 1) * TOK)
        info = q_ref[TOK:PAY, :].astype(F32)
        for h in range(GROUP):
            qs[h, toks, :] = q_ref[0:TOK, h * HD : (h + 1) * HD]
            gs[h, toks, :] = q_ref[0:TOK, WIDE + h * HD : WIDE + (h + 1) * HD]
            high = info[0:1, h * TOK : (h + 1) * TOK]
            low = info[0:1, (GROUP + h) * TOK : (GROUP + h + 1) * TOK]
            delta[h : h + 1, toks] = high + low
    dq[...] = dq_in[...] if last else jnp.zeros_like(dq)

    top = functools.reduce(jnp.maximum, [all_ref[y, 0:GROUP] for y in range(YS)])
    total = sum(
        all_ref[y, GROUP : 2 * GROUP] * jnp.exp2((all_ref[y, 0:GROUP] - top) * EXP2)
        for y in range(YS)
    )
    for step in range(STEPS):
        rows = slice(step * KT, (step + 1) * KT)
        peaks = jnp.concatenate([st_ref[step, 0:GROUP] for st_ref in st_refs], axis=1)
        weight = jnp.exp2((peaks - top) * EXP2) / total
        pair = [kv_ref[2 * step + b, 0:TOK] for b in range(2)]
        keys = jnp.concatenate([part[:, 0:HD] for part in pair], axis=0)
        values = jnp.concatenate([part[:, HD : 2 * HD] for part in pair], axis=0)
        dk = jnp.zeros((KT, HD), F32)
        dv = jnp.zeros((KT, HD), F32)
        for h in range(GROUP):
            dp = dot(values, gs[h], NT)
            widths = [st_ref.shape[2] for st_ref in st_refs]
            p = jnp.concatenate(
                [ref[rows, h * w : (h + 1) * w] for ref, w in zip(p_refs, widths)], axis=1
            )
            p = p.astype(F32) * weight[h : h + 1]
            ds = (p * (dp - delta[h : h + 1, :])).astype(BF16)
            dv = dv + dot(p.astype(BF16), gs[h])
            dk = dk + dot(ds, qs[h])
            dq[h] += dot(keys, ds, TN)
        dk = dk * SCALE
        for b in range(2):
            half = slice(b * TOK, (b + 1) * TOK)
            dkv_ref[2 * step + b, :, 0:HD] = dk[half].astype(dkv_ref.dtype)
            dkv_ref[2 * step + b, :, HD : 2 * HD] = dv[half].astype(dkv_ref.dtype)

    if last:
        for x, out in enumerate((own_ref, send1, send2, send3)):
            for h in range(GROUP):
                part = dq[h, :, x * TOK : (x + 1) * TOK].T * SCALE
                out[:, h * HD : (h + 1) * HD] = part.astype(out.dtype)


def shape_of(shape, dtype):
    return jax.ShapeDtypeStruct(shape, dtype)


def params(limit=VMEM_LIMIT):
    return pltpu.CompilerParams(vmem_limit_bytes=limit << 20)


def pack(order, seg, q, k, v, o, g):
    hbm = pl.BlockSpec(memory_space=pltpu.HBM)
    vm = pl.BlockSpec(memory_space=pltpu.VMEM)
    return pl.pallas_call(
        pack_kernel,
        out_shape=(shape_of((ZS, PAY, 2 * HD), BF16), shape_of((PAY, 2 * WIDE), BF16)),
        in_specs=[hbm] * 7,
        out_specs=(hbm, vm),
        scratch_shapes=[
            pltpu.SMEM((2,), jnp.int32),
            pltpu.VMEM((1, TOK), jnp.int32),
            pltpu.VMEM((PAY, 2 * HD), BF16),
            pltpu.VMEM((TOK, GROUP * HD), BF16),
            pltpu.SemaphoreType.DMA((7,)),
            pltpu.SemaphoreType.DMA((ZS,)),
        ],
        compiler_params=params(60),
        name="pack",
    )(order, seg, q, k, v, o, g)


STEPS = ZS // 2
VMEM = pl.BlockSpec(memory_space=pltpu.VMEM)
SMEM = pl.BlockSpec(memory_space=pltpu.SMEM)
STATS = (2 * GROUP, QT)
STATED = {"near": 69 * 10**8, "near_twin": 10**8, "far": 10**8, "far_twin": 10**8, "grads": 6 * 10**9}


def cost(kind):
    return pl.CostEstimate(flops=STATED[kind], bytes_accessed=1 << 16, transcendentals=0)


def scores(kind, kv, queries, prev=None, place=None):
    width = len(queries) * TOK
    args = [kv, *queries]
    in_specs = [VMEM] * len(args)
    out_shape = [
        shape_of((ZS * TOK, GROUP * width), BF16),
        shape_of((STEPS, 2 * GROUP, width), F32),
    ]
    if prev is not None:
        args += [place, *prev]
        in_specs += [SMEM, VMEM, VMEM, VMEM]
        out_shape.append(shape_of((YS, *STATS), F32))
    return pl.pallas_call(
        functools.partial(score_kernel, len(queries), prev is not None),
        in_specs=in_specs,
        out_specs=[VMEM] * len(out_shape),
        out_shape=out_shape,
        scratch_shapes=[
            pltpu.VMEM((GROUP, width, HD), BF16),
            pltpu.VMEM((8, width), F32),
            pltpu.VMEM((2, KT, width), F32),
        ],
        compiler_params=params(),
        cost_estimate=cost(kind),
        name="scores_" + kind,
    )(*args)


def grads(kv, probs, stats, all_stats, queries, dq_in=None):
    last = dq_in is not None
    dq_shape = (GROUP, HD, QT)
    args = [kv, all_stats, *probs, *stats, *queries]
    out_shape = [shape_of((ZS, TOK, 2 * HD), F32 if last else BF16)]
    scratch = [
        pltpu.VMEM((GROUP, QT, HD), BF16),
        pltpu.VMEM((GROUP, QT, HD), BF16),
        pltpu.VMEM((8, QT), F32),
    ]
    if last:
        args.append(dq_in)
        out_shape += [shape_of((TOK, WIDE), F32)] + [shape_of((TOK, WIDE), BF16)] * (YS - 1)
        scratch.append(pltpu.VMEM(dq_shape, F32))
    else:
        out_shape.append(shape_of(dq_shape, F32))
    return pl.pallas_call(
        functools.partial(grad_kernel, last, len(probs)),
        in_specs=[VMEM] * len(args),
        out_specs=[VMEM] * len(out_shape),
        out_shape=out_shape,
        scratch_shapes=scratch,
        compiler_params=params(),
        cost_estimate=cost("grads"),
        name="grads",
    )(*args)


def per_device(query, key_rows, value_rows, output, grad_out, block_order, segment):
    n = lax.axis_size("ctx")
    key_groups = [[r + 8 * z for z in range(ZS)] for r in range(ZS)]
    tile_groups = [[c + 8 * z + bits for bits in TILE] for z in range(ZS) for c in range(2)]

    def swap(x, bits):
        return lax.ppermute(x, "ctx", [(i, i ^ bits) for i in range(n)])

    def exchange(x, groups):
        return lax.all_to_all(x, "ctx", 0, 0, tiled=True, axis_index_groups=groups)

    kv_pay, q_pay = pack(
        block_order, segment.reshape(1, TOK), query, key_rows, value_rows, output, grad_out
    )
    kv_own = exchange(kv_pay, key_groups)
    q_far, q_near = swap(q_pay, TILE[2]), swap(q_pay, TILE[1])
    queries = [q_pay, q_near, q_far, swap(q_far, TILE[1])]
    kv_twin = swap(kv_own, 1)
    index = lax.axis_index("ctx").astype(jnp.int32)
    place = (index >> 1 & (YS - 1)).reshape(1)
    near, far = queries[:3], queries[3:]
    p_near, st_near = scores("near", kv_own, near)
    p_near_twin, st_near_twin = scores("near_twin", kv_twin, near)
    st_near_twin, far = lax.optimization_barrier((st_near_twin, far))
    queries = near + far
    p_far, st_far = scores("far", kv_own, far)
    prev = (st_near, st_near_twin, st_far)
    p_far_twin, st_far_twin, stats = scores("far_twin", kv_twin, far, prev, place)
    all_stats = exchange(stats, tile_groups)
    dkv_twin, dq = grads(
        kv_twin, [p_near_twin, p_far_twin], [st_near_twin, st_far_twin], all_stats, queries
    )
    dkv_back = swap(dkv_twin, 1)
    dkv_own, dq_own, *dq_send = grads(
        kv_own, [p_near, p_far], [st_near, st_far], all_stats, queries, dq
    )
    dkv = (dkv_own + dkv_back.astype(F32)).astype(BF16)
    dkv_all = exchange(dkv, key_groups)
    dq_parts = [swap(part, bits) for part, bits in zip(dq_send[::-1], TILE[:0:-1])]
    grad_query = dq_own + sum(part.astype(F32) for part in dq_parts)
    grad_kv = jnp.sum(dkv_all.astype(F32), axis=0).astype(BF16)
    return grad_query.astype(BF16), grad_kv[:, 0:HD], grad_kv[:, HD : 2 * HD]


def solution(mesh):
    both = P("ctx", "kvh")
    return jax.shard_map(
        per_device,
        mesh=mesh,
        in_specs=(both, both, both, both, both, P("ctx"), P("ctx")),
        out_specs=(both, both, both),
        check_vma=False,
    )
```

```python
import functools

import jax
import jax.numpy as jnp
from jax import lax
from jax.experimental import pallas as pl
from jax.experimental.pallas import tpu as pltpu
from jax.sharding import PartitionSpec as P

HEADS = 32
KV_HEADS = 8
HD = 128
GROUP = HEADS // KV_HEADS
BLK = 64
TOKENS = 8192
TOK = 128
EXTRA = 16
PAY = TOK + EXTRA
YS = 4
TILE = (0, 2, 4, 6)
ZS = 8
WIDE = GROUP * HD
QT = YS * TOK
KT = 2 * TOK
SCALE = HD**-0.5
EXP2 = SCALE * 1.4426950408889634
MASKED = -1e30
FLOOR = -1e25
F32 = jnp.float32
BF16 = jnp.bfloat16
VMEM_LIMIT = 24

NT = (((1,), (1,)), ((), ()))
TN = (((0,), (0,)), ((), ()))


def dot(a, b, dims=(((1,), (0,)), ((), ()))):
    return lax.dot_general(a, b, dims, preferred_element_type=F32)


def pack_kernel(
    order_hbm, seg_hbm, q_hbm, k_hbm, v_hbm, o_hbm, g_hbm, kvp_hbm, qp_hbm,
    order_ref, seg_ref, kv_ref, o_ref, g_ref, q_ref, extra_ref, in_sems, out_sems,
):
    moves = (
        (order_hbm, order_ref),
        (seg_hbm, seg_ref),
        (k_hbm, kv_ref.at[0:TOK, 0:HD]),
        (v_hbm, kv_ref.at[0:TOK, HD : 2 * HD]),
        (o_hbm, o_ref),
        (g_hbm, g_ref),
        (q_hbm, q_ref),
    )
    copies = [
        pltpu.make_async_copy(src, dst, in_sems.at[i]) for i, (src, dst) in enumerate(moves)
    ]
    for copy in copies:
        copy.start()
    for copy in copies[:4]:
        copy.wait()
    lane = lax.broadcasted_iota(jnp.int32, (1, TOK), 1)
    block = jnp.where(lane < BLK, order_ref[0], order_ref[1]).astype(F32)
    doc = seg_ref[...].astype(F32)
    kv_extra = jnp.concatenate([doc, block], axis=1)
    kv_ref[TOK:PAY, :] = jnp.broadcast_to(kv_extra, (EXTRA, 2 * HD)).astype(BF16)
    outs = [
        pltpu.make_async_copy(kv_ref, kvp_hbm.at[z], out_sems.at[z]) for z in range(ZS)
    ]
    for copy in outs:
        copy.start()
    for copy in copies[4:]:
        copy.wait()
    for src, dst in ((q_ref, qp_hbm.at[0:TOK, 0:WIDE]), (g_ref, qp_hbm.at[0:TOK, WIDE : 2 * WIDE])):
        outs.append(pltpu.make_async_copy(src, dst, out_sems.at[len(outs)]))
        outs[-1].start()
    highs, lows = [], []
    for h in range(GROUP):
        cols = slice(h * HD, (h + 1) * HD)
        prod = g_ref[:, cols].astype(F32) * o_ref[:, cols].astype(F32)
        delta = jnp.sum(prod.T, axis=0, keepdims=True)
        high = delta.astype(BF16).astype(F32)
        highs.append(high)
        lows.append(delta - high)
    zero = jnp.zeros_like(doc)
    first = jnp.concatenate(highs + lows, axis=1)
    second = jnp.concatenate([doc, block] + [zero] * 6, axis=1)
    row = lax.broadcasted_iota(jnp.int32, (EXTRA, 2 * WIDE), 0)
    extra_ref[...] = jnp.where(row == 0, first, second).astype(BF16)
    outs.append(pltpu.make_async_copy(extra_ref, qp_hbm.at[TOK:PAY], out_sems.at[len(outs)]))
    outs[-1].start()
    for copy in outs:
        copy.wait()


def code_of(doc, block):
    lane = lax.broadcasted_iota(jnp.int32, doc.shape, 1)
    within = jnp.where(lane < BLK, lane, lane - BLK).astype(F32)
    return doc * TOKENS + block * BLK + within


def score_kernel(n_q, last, kv_ref, *refs):
    q_refs, refs = refs[:n_q], refs[n_q:]
    if last:
        place_ref, near_own, near_twin, far_own, pt_ref, st_ref, fin_ref, qs, code, bias = refs
    else:
        pt_ref, st_ref, qs, code, bias = refs
    width = n_q * TOK
    for x, q_ref in enumerate(q_refs):
        toks = slice(x * TOK, (x + 1) * TOK)
        for h in range(GROUP):
            qs[h, toks, :] = q_ref[0:TOK, h * HD : (h + 1) * HD]
        info = q_ref[TOK:PAY, :].astype(F32)
        doc, block = info[1:2, 0:TOK], info[1:2, TOK : 2 * TOK]
        code[0:1, toks] = code_of(doc, block)
        code[1:2, toks] = doc * TOKENS

    for step in range(STEPS):
        for b in range(2):
            info = kv_ref[2 * step + b, TOK:PAY, :].astype(F32)
            key_code = code_of(info[0:1, 0:TOK], info[0:1, TOK : 2 * TOK])
            key_code = jnp.broadcast_to(key_code, (TOK, TOK)).T
            for x in range(n_q):
                toks = slice(x * TOK, (x + 1) * TOK)
                ok = (key_code <= code[0:1, toks]) & (key_code >= code[1:2, toks])
                bias[step % 2, b * TOK : (b + 1) * TOK, toks] = jnp.where(ok, 0.0, MASKED)
        rows = slice(step * KT, (step + 1) * KT)
        keys = jnp.concatenate([kv_ref[2 * step + b, 0:TOK, 0:HD] for b in range(2)], axis=0)
        for h in range(GROUP):
            s = dot(keys, qs[h], NT) + bias[step % 2]
            peak = jnp.maximum(jnp.max(s, axis=0, keepdims=True), FLOOR)
            p = jnp.exp2((s - peak) * EXP2)
            st_ref[step, h : h + 1, :] = peak
            st_ref[step, GROUP + h : GROUP + h + 1, :] = jnp.sum(p, axis=0, keepdims=True)
            pt_ref[rows, h * width : (h + 1) * width] = p.astype(BF16)
    if last:
        tiles = [
            jnp.concatenate([near_ref[t], far_ref[t]], axis=1)
            for near_ref, far_ref in ((near_own, far_own), (near_twin, st_ref))
            for t in range(STEPS)
        ]
        top = functools.reduce(jnp.maximum, [t[0:GROUP] for t in tiles])
        total = sum(t[GROUP:] * jnp.exp2((t[0:GROUP] - top) * EXP2) for t in tiles)
        for d in range(YS):
            for x in range(YS):
                to, of = slice(x * TOK, (x + 1) * TOK), slice((x ^ d) * TOK, ((x ^ d) + 1) * TOK)
                fin_ref[place_ref[0] ^ d, 0:GROUP, to] = top[:, of]
                fin_ref[place_ref[0] ^ d, GROUP : 2 * GROUP, to] = total[:, of]


def grad_kernel(last, n_parts, kv_ref, all_ref, *refs):
    p_refs, refs = refs[:n_parts], refs[n_parts:]
    st_refs, refs = refs[:n_parts], refs[n_parts:]
    q_refs, refs = refs[:YS], refs[YS:]
    if last:
        dq_in, dkv_ref, own_ref, send1, send2, send3, qs, gs, delta, dq = refs
    else:
        dkv_ref, dq, qs, gs, delta = refs
    for x, q_ref in enumerate(q_refs):
        toks = slice(x * TOK, (x + 1) * TOK)
        info = q_ref[TOK:PAY, :].astype(F32)
        for h in range(GROUP):
            qs[h, toks, :] = q_ref[0:TOK, h * HD : (h + 1) * HD]
            gs[h, toks, :] = q_ref[0:TOK, WIDE + h * HD : WIDE + (h + 1) * HD]
            high = info[0:1, h * TOK : (h + 1) * TOK]
            low = info[0:1, (GROUP + h) * TOK : (GROUP + h + 1) * TOK]
            delta[h : h + 1, toks] = high + low
    dq[...] = dq_in[...] if last else jnp.zeros_like(dq)

    top = functools.reduce(jnp.maximum, [all_ref[y, 0:GROUP] for y in range(YS)])
    total = sum(
        all_ref[y, GROUP : 2 * GROUP] * jnp.exp2((all_ref[y, 0:GROUP] - top) * EXP2)
        for y in range(YS)
    )
    for first in range(0, STEPS, 2):
        tiles = (first, first + 1)
        weights = []
        for tile in tiles:
            peaks = jnp.concatenate([st_ref[tile, 0:GROUP] for st_ref in st_refs], axis=1)
            weights.append(jnp.exp2((peaks - top) * EXP2) / total)
        blocks = range(2 * first, 2 * first + 4)
        keys = jnp.concatenate([kv_ref[b, 0:TOK, 0:HD] for b in blocks], axis=0)
        values = jnp.concatenate([kv_ref[b, 0:TOK, HD : 2 * HD] for b in blocks], axis=0)
        dk = jnp.zeros((2 * KT, HD), F32)
        dv = jnp.zeros((2 * KT, HD), F32)
        for h in range(GROUP):
            dp = dot(values, gs[h], NT)
            parts = []
            for tile, weight in zip(tiles, weights):
                rows = slice(tile * KT, (tile + 1) * KT)
                widths = [st_ref.shape[2] for st_ref in st_refs]
                part = jnp.concatenate(
                    [ref[rows, h * w : (h + 1) * w] for ref, w in zip(p_refs, widths)], axis=1
                )
                parts.append(part.astype(F32) * weight[h : h + 1])
            p = jnp.concatenate(parts, axis=0)
            ds = (p * (dp - delta[h : h + 1, :])).astype(BF16)
            dv = dv + dot(p.astype(BF16), gs[h])
            dk = dk + dot(ds, qs[h])
            dq[h] += dot(keys, ds, TN)
        dk = dk * SCALE
        for i, b in enumerate(blocks):
            rows = slice(i * TOK, (i + 1) * TOK)
            dkv_ref[b, :, 0:HD] = dk[rows].astype(dkv_ref.dtype)
            dkv_ref[b, :, HD : 2 * HD] = dv[rows].astype(dkv_ref.dtype)

    if last:
        for x, out in enumerate((own_ref, send1, send2, send3)):
            for h in range(GROUP):
                part = dq[h, :, x * TOK : (x + 1) * TOK].T * SCALE
                out[:, h * HD : (h + 1) * HD] = part.astype(out.dtype)


def shape_of(shape, dtype):
    return jax.ShapeDtypeStruct(shape, dtype)


def params(limit=VMEM_LIMIT):
    return pltpu.CompilerParams(vmem_limit_bytes=limit << 20)


def pack(order, seg, q, k, v, o, g):
    hbm = pl.BlockSpec(memory_space=pltpu.HBM)
    return pl.pallas_call(
        pack_kernel,
        out_shape=(shape_of((ZS, PAY, 2 * HD), BF16), shape_of((PAY, 2 * WIDE), BF16)),
        in_specs=[hbm] * 7,
        out_specs=(hbm, hbm),
        scratch_shapes=[
            pltpu.SMEM((2,), jnp.int32),
            pltpu.VMEM((1, TOK), jnp.int32),
            pltpu.VMEM((PAY, 2 * HD), BF16),
            pltpu.VMEM((TOK, WIDE), BF16),
            pltpu.VMEM((TOK, WIDE), BF16),
            pltpu.VMEM((TOK, WIDE), BF16),
            pltpu.VMEM((EXTRA, 2 * WIDE), BF16),
            pltpu.SemaphoreType.DMA((7,)),
            pltpu.SemaphoreType.DMA((ZS + 3,)),
        ],
        compiler_params=params(60),
        name="pack",
    )(order, seg, q, k, v, o, g)


STEPS = ZS // 2
VMEM = pl.BlockSpec(memory_space=pltpu.VMEM)
SMEM = pl.BlockSpec(memory_space=pltpu.SMEM)
STATS = (2 * GROUP, QT)
STATED = {"near": 69 * 10**8, "near_twin": 10**8, "far": 10**8, "far_twin": 10**8, "grads": 6 * 10**9}


def cost(kind):
    return pl.CostEstimate(flops=STATED[kind], bytes_accessed=1 << 16, transcendentals=0)


def scores(kind, kv, queries, prev=None, place=None):
    width = len(queries) * TOK
    args = [kv, *queries]
    in_specs = [VMEM] * len(args)
    out_shape = [
        shape_of((ZS * TOK, GROUP * width), BF16),
        shape_of((STEPS, 2 * GROUP, width), F32),
    ]
    if prev is not None:
        args += [place, *prev]
        in_specs += [SMEM, VMEM, VMEM, VMEM]
        out_shape.append(shape_of((YS, *STATS), F32))
    return pl.pallas_call(
        functools.partial(score_kernel, len(queries), prev is not None),
        in_specs=in_specs,
        out_specs=[VMEM] * len(out_shape),
        out_shape=out_shape,
        scratch_shapes=[
            pltpu.VMEM((GROUP, width, HD), BF16),
            pltpu.VMEM((8, width), F32),
            pltpu.VMEM((2, KT, width), F32),
        ],
        compiler_params=params(),
        cost_estimate=cost(kind),
        name="scores_" + kind,
    )(*args)


def grads(kv, probs, stats, all_stats, queries, dq_in=None):
    last = dq_in is not None
    dq_shape = (GROUP, HD, QT)
    args = [kv, all_stats, *probs, *stats, *queries]
    out_shape = [shape_of((ZS, TOK, 2 * HD), F32 if last else BF16)]
    scratch = [
        pltpu.VMEM((GROUP, QT, HD), BF16),
        pltpu.VMEM((GROUP, QT, HD), BF16),
        pltpu.VMEM((8, QT), F32),
    ]
    if last:
        args.append(dq_in)
        out_shape += [shape_of((TOK, WIDE), F32)] + [shape_of((TOK, WIDE), BF16)] * (YS - 1)
        scratch.append(pltpu.VMEM(dq_shape, F32))
    else:
        out_shape.append(shape_of(dq_shape, F32))
    return pl.pallas_call(
        functools.partial(grad_kernel, last, len(probs)),
        in_specs=[VMEM] * len(args),
        out_specs=[VMEM] * len(out_shape),
        out_shape=out_shape,
        scratch_shapes=scratch,
        compiler_params=params(),
        cost_estimate=cost("grads"),
        name="grads",
    )(*args)


def per_device(query, key_rows, value_rows, output, grad_out, block_order, segment):
    n = lax.axis_size("ctx")
    key_groups = [[r + 8 * z for z in range(ZS)] for r in range(ZS)]
    tile_groups = [[c + 8 * z + bits for bits in TILE] for z in range(ZS) for c in range(2)]

    def swap(x, bits):
        return lax.ppermute(x, "ctx", [(i, i ^ bits) for i in range(n)])

    def exchange(x, groups):
        return lax.all_to_all(x, "ctx", 0, 0, tiled=True, axis_index_groups=groups)

    kv_pay, q_pay = pack(
        block_order, segment.reshape(1, TOK), query, key_rows, value_rows, output, grad_out
    )
    kv_own = exchange(kv_pay, key_groups)
    q_far, q_near = swap(q_pay, TILE[2]), swap(q_pay, TILE[1])
    queries = [q_pay, q_near, q_far, swap(q_far, TILE[1])]
    kv_twin = swap(kv_own, 1)
    index = lax.axis_index("ctx").astype(jnp.int32)
    place = (index >> 1 & (YS - 1)).reshape(1)
    near, far = queries[:3], queries[3:]
    p_near, st_near = scores("near", kv_own, near)
    p_near_twin, st_near_twin = scores("near_twin", kv_twin, near)
    st_near_twin, far = lax.optimization_barrier((st_near_twin, far))
    queries = near + far
    p_far, st_far = scores("far", kv_own, far)
    prev = (st_near, st_near_twin, st_far)
    p_far_twin, st_far_twin, stats = scores("far_twin", kv_twin, far, prev, place)
    all_stats = exchange(stats, tile_groups)
    dkv_twin, dq = grads(
        kv_twin, [p_near_twin, p_far_twin], [st_near_twin, st_far_twin], all_stats, queries
    )
    dkv_back = swap(dkv_twin, 1)
    dkv_own, dq_own, *dq_send = grads(
        kv_own, [p_near, p_far], [st_near, st_far], all_stats, queries, dq
    )
    dkv = (dkv_own + dkv_back.astype(F32)).astype(BF16)
    dkv_all = exchange(dkv, key_groups)
    dq_parts = [swap(part, bits) for part, bits in zip(dq_send[::-1], TILE[:0:-1])]
    grad_query = dq_own + sum(part.astype(F32) for part in dq_parts)
    grad_kv = jnp.sum(dkv_all.astype(F32), axis=0).astype(BF16)
    return grad_query.astype(BF16), grad_kv[:, 0:HD], grad_kv[:, HD : 2 * HD]


def solution(mesh):
    both = P("ctx", "kvh")
    return jax.shard_map(
        per_device,
        mesh=mesh,
        in_specs=(both, both, both, both, both, P("ctx"), P("ctx")),
        out_specs=(both, both, both),
        check_vma=False,
    )
```

```python
import functools

import jax
import jax.numpy as jnp
from jax import lax
from jax.experimental import pallas as pl
from jax.experimental.pallas import tpu as pltpu
from jax.sharding import PartitionSpec as P

HEADS = 32
KV_HEADS = 8
HD = 128
GROUP = HEADS // KV_HEADS
BLK = 64
TOKENS = 8192
TOK = 128
EXTRA = 16
PAY = TOK + EXTRA
YS = 4
TILE = (0, 2, 4, 6)
ZS = 8
WIDE = GROUP * HD
QT = YS * TOK
KT = 2 * TOK
SCALE = HD**-0.5
EXP2 = SCALE * 1.4426950408889634
MASKED = -1e30
FLOOR = -1e25
F32 = jnp.float32
BF16 = jnp.bfloat16
VMEM_LIMIT = 24

NT = (((1,), (1,)), ((), ()))
TN = (((0,), (0,)), ((), ()))


def dot(a, b, dims=(((1,), (0,)), ((), ()))):
    return lax.dot_general(a, b, dims, preferred_element_type=F32)


def pack_kernel(
    order_hbm, seg_hbm, q_hbm, k_hbm, v_hbm, o_hbm, g_hbm, kvp_hbm, qp_hbm,
    order_ref, seg_ref, kv_ref, o_ref, g_ref, q_ref, extra_ref, in_sems, out_sems,
):
    moves = (
        (order_hbm, order_ref),
        (seg_hbm, seg_ref),
        (k_hbm, kv_ref.at[0:TOK, 0:HD]),
        (v_hbm, kv_ref.at[0:TOK, HD : 2 * HD]),
        (o_hbm, o_ref),
        (g_hbm, g_ref),
        (q_hbm, q_ref),
    )
    copies = [
        pltpu.make_async_copy(src, dst, in_sems.at[i]) for i, (src, dst) in enumerate(moves)
    ]
    for copy in copies:
        copy.start()
    for copy in copies[:4]:
        copy.wait()
    lane = lax.broadcasted_iota(jnp.int32, (1, TOK), 1)
    block = jnp.where(lane < BLK, order_ref[0], order_ref[1]).astype(F32)
    doc = seg_ref[...].astype(F32)
    kv_extra = jnp.concatenate([doc, block], axis=1)
    kv_ref[TOK:PAY, :] = jnp.broadcast_to(kv_extra, (EXTRA, 2 * HD)).astype(BF16)
    outs = [
        pltpu.make_async_copy(kv_ref, kvp_hbm.at[z], out_sems.at[z]) for z in range(ZS)
    ]
    for copy in outs:
        copy.start()
    for copy in copies[4:]:
        copy.wait()
    for src, dst in ((q_ref, qp_hbm.at[0:TOK, 0:WIDE]), (g_ref, qp_hbm.at[0:TOK, WIDE : 2 * WIDE])):
        outs.append(pltpu.make_async_copy(src, dst, out_sems.at[len(outs)]))
        outs[-1].start()
    highs, lows = [], []
    for h in range(GROUP):
        cols = slice(h * HD, (h + 1) * HD)
        prod = g_ref[:, cols].astype(F32) * o_ref[:, cols].astype(F32)
        delta = jnp.sum(prod.T, axis=0, keepdims=True)
        high = delta.astype(BF16).astype(F32)
        highs.append(high)
        lows.append(delta - high)
    zero = jnp.zeros_like(doc)
    first = jnp.concatenate(highs + lows, axis=1)
    second = jnp.concatenate([doc, block] + [zero] * 6, axis=1)
    row = lax.broadcasted_iota(jnp.int32, (EXTRA, 2 * WIDE), 0)
    extra_ref[...] = jnp.where(row == 0, first, second).astype(BF16)
    outs.append(pltpu.make_async_copy(extra_ref, qp_hbm.at[TOK:PAY], out_sems.at[len(outs)]))
    outs[-1].start()
    for copy in outs:
        copy.wait()


def code_of(doc, block):
    lane = lax.broadcasted_iota(jnp.int32, doc.shape, 1)
    within = jnp.where(lane < BLK, lane, lane - BLK).astype(F32)
    return doc * TOKENS + block * BLK + within


def score_kernel(n_q, last, kv_ref, *refs):
    q_refs, refs = refs[:n_q], refs[n_q:]
    if last:
        place_ref, near_own, near_twin, far_own, pt_ref, st_ref, fin_ref, qs, code, bias = refs
    else:
        pt_ref, st_ref, qs, code, bias = refs
    width = n_q * TOK
    for x, q_ref in enumerate(q_refs):
        toks = slice(x * TOK, (x + 1) * TOK)
        for h in range(GROUP):
            qs[h, toks, :] = q_ref[0:TOK, h * HD : (h + 1) * HD]
        info = q_ref[TOK:PAY, :].astype(F32)
        doc, block = info[1:2, 0:TOK], info[1:2, TOK : 2 * TOK]
        code[0:1, toks] = code_of(doc, block)
        code[1:2, toks] = doc * TOKENS

    for step in range(STEPS):
        for b in range(2):
            info = kv_ref[2 * step + b, TOK:PAY, :].astype(F32)
            key_code = code_of(info[0:1, 0:TOK], info[0:1, TOK : 2 * TOK])
            key_code = jnp.broadcast_to(key_code, (TOK, TOK)).T
            for x in range(n_q):
                toks = slice(x * TOK, (x + 1) * TOK)
                ok = (key_code <= code[0:1, toks]) & (key_code >= code[1:2, toks])
                bias[step % 2, b * TOK : (b + 1) * TOK, toks] = jnp.where(ok, 0.0, MASKED)
        rows = slice(step * KT, (step + 1) * KT)
        keys = jnp.concatenate([kv_ref[2 * step + b, 0:TOK, 0:HD] for b in range(2)], axis=0)
        for h in range(GROUP):
            s = dot(keys, qs[h], NT) + bias[step % 2]
            peak = jnp.maximum(jnp.max(s, axis=0, keepdims=True), FLOOR)
            p = jnp.exp2((s - peak) * EXP2)
            st_ref[step, h : h + 1, :] = peak
            st_ref[step, GROUP + h : GROUP + h + 1, :] = jnp.sum(p, axis=0, keepdims=True)
            pt_ref[rows, h * width : (h + 1) * width] = p.astype(BF16)
    if last:
        tiles = [
            jnp.concatenate([near_ref[t], far_ref[t]], axis=1)
            for near_ref, far_ref in ((near_own, far_own), (near_twin, st_ref))
            for t in range(STEPS)
        ]
        top = functools.reduce(jnp.maximum, [t[0:GROUP] for t in tiles])
        total = sum(t[GROUP:] * jnp.exp2((t[0:GROUP] - top) * EXP2) for t in tiles)
        for d in range(YS):
            for x in range(YS):
                to, of = slice(x * TOK, (x + 1) * TOK), slice((x ^ d) * TOK, ((x ^ d) + 1) * TOK)
                fin_ref[place_ref[0] ^ d, 0:GROUP, to] = top[:, of]
                fin_ref[place_ref[0] ^ d, GROUP : 2 * GROUP, to] = total[:, of]


def grad_kernel(last, n_parts, kv_ref, all_ref, *refs):
    p_refs, refs = refs[:n_parts], refs[n_parts:]
    st_refs, refs = refs[:n_parts], refs[n_parts:]
    q_refs, refs = refs[:YS], refs[YS:]
    if last:
        dq_in, dkv_ref, own_ref, send1, send2, send3, qs, gs, delta, dq = refs
    else:
        dkv_ref, dq, qs, gs, delta = refs
    for x, q_ref in enumerate(q_refs):
        toks = slice(x * TOK, (x + 1) * TOK)
        info = q_ref[TOK:PAY, :].astype(F32)
        for h in range(GROUP):
            qs[h, toks, :] = q_ref[0:TOK, h * HD : (h + 1) * HD]
            gs[h, toks, :] = q_ref[0:TOK, WIDE + h * HD : WIDE + (h + 1) * HD]
            high = info[0:1, h * TOK : (h + 1) * TOK]
            low = info[0:1, (GROUP + h) * TOK : (GROUP + h + 1) * TOK]
            delta[h : h + 1, toks] = high + low
    dq[...] = dq_in[...] if last else jnp.zeros_like(dq)

    top = functools.reduce(jnp.maximum, [all_ref[y, 0:GROUP] for y in range(YS)])
    total = sum(
        all_ref[y, GROUP : 2 * GROUP] * jnp.exp2((all_ref[y, 0:GROUP] - top) * EXP2)
        for y in range(YS)
    )
    for first in range(0, STEPS, 2):
        tiles = (first, first + 1)
        weights = []
        for tile in tiles:
            peaks = jnp.concatenate([st_ref[tile, 0:GROUP] for st_ref in st_refs], axis=1)
            weights.append(jnp.exp2((peaks - top) * EXP2) / total)
        blocks = range(2 * first, 2 * first + 4)
        keys = jnp.concatenate([kv_ref[b, 0:TOK, 0:HD] for b in blocks], axis=0)
        values = jnp.concatenate([kv_ref[b, 0:TOK, HD : 2 * HD] for b in blocks], axis=0)
        dk = jnp.zeros((2 * KT, HD), F32)
        dv = jnp.zeros((2 * KT, HD), F32)
        for h in range(GROUP):
            dp = dot(values, gs[h], NT)
            parts = []
            for tile, weight in zip(tiles, weights):
                rows = slice(tile * KT, (tile + 1) * KT)
                widths = [st_ref.shape[2] for st_ref in st_refs]
                part = jnp.concatenate(
                    [ref[rows, h * w : (h + 1) * w] for ref, w in zip(p_refs, widths)], axis=1
                )
                parts.append(part.astype(F32) * weight[h : h + 1])
            p = jnp.concatenate(parts, axis=0)
            ds = (p * (dp - delta[h : h + 1, :])).astype(BF16)
            dv = dv + dot(p.astype(BF16), gs[h])
            dk = dk + dot(ds, qs[h])
            dq[h] += dot(keys, ds, TN)
        dk = dk * SCALE
        for i, b in enumerate(blocks):
            rows = slice(i * TOK, (i + 1) * TOK)
            dkv_ref[b, :, 0:HD] = dk[rows].astype(dkv_ref.dtype)
            dkv_ref[b, :, HD : 2 * HD] = dv[rows].astype(dkv_ref.dtype)

    if last:
        for x, out in enumerate((own_ref, send1, send2, send3)):
            for h in range(GROUP):
                part = dq[h, :, x * TOK : (x + 1) * TOK].T * SCALE
                out[:, h * HD : (h + 1) * HD] = part.astype(out.dtype)


def shape_of(shape, dtype):
    return jax.ShapeDtypeStruct(shape, dtype)


def params(limit=VMEM_LIMIT):
    return pltpu.CompilerParams(vmem_limit_bytes=limit << 20)


def pack(order, seg, q, k, v, o, g):
    hbm = pl.BlockSpec(memory_space=pltpu.HBM)
    return pl.pallas_call(
        pack_kernel,
        out_shape=(shape_of((ZS, PAY, 2 * HD), BF16), shape_of((PAY, 2 * WIDE), BF16)),
        in_specs=[hbm] * 7,
        out_specs=(hbm, hbm),
        scratch_shapes=[
            pltpu.SMEM((2,), jnp.int32),
            pltpu.VMEM((1, TOK), jnp.int32),
            pltpu.VMEM((PAY, 2 * HD), BF16),
            pltpu.VMEM((TOK, WIDE), BF16),
            pltpu.VMEM((TOK, WIDE), BF16),
            pltpu.VMEM((TOK, WIDE), BF16),
            pltpu.VMEM((EXTRA, 2 * WIDE), BF16),
            pltpu.SemaphoreType.DMA((7,)),
            pltpu.SemaphoreType.DMA((ZS + 3,)),
        ],
        compiler_params=params(60),
        name="pack",
    )(order, seg, q, k, v, o, g)


STEPS = ZS // 2
VMEM = pl.BlockSpec(memory_space=pltpu.VMEM)
SMEM = pl.BlockSpec(memory_space=pltpu.SMEM)
STATS = (2 * GROUP, QT)
STATED = {"near": 46 * 10**8, "near_twin": 10**8, "far": 10**8, "far_twin": 10**8, "grads": 6 * 10**9}


def cost(kind):
    return pl.CostEstimate(flops=STATED[kind], bytes_accessed=1 << 16, transcendentals=0)


def scores(kind, kv, queries, prev=None, place=None):
    width = len(queries) * TOK
    args = [kv, *queries]
    in_specs = [VMEM] * len(args)
    out_shape = [
        shape_of((ZS * TOK, GROUP * width), BF16),
        shape_of((STEPS, 2 * GROUP, width), F32),
    ]
    if prev is not None:
        args += [place, *prev]
        in_specs += [SMEM, VMEM, VMEM, VMEM]
        out_shape.append(shape_of((YS, *STATS), F32))
    return pl.pallas_call(
        functools.partial(score_kernel, len(queries), prev is not None),
        in_specs=in_specs,
        out_specs=[VMEM] * len(out_shape),
        out_shape=out_shape,
        scratch_shapes=[
            pltpu.VMEM((GROUP, width, HD), BF16),
            pltpu.VMEM((8, width), F32),
            pltpu.VMEM((2, KT, width), F32),
        ],
        compiler_params=params(),
        cost_estimate=cost(kind),
        name="scores_" + kind,
    )(*args)


def grads(kv, probs, stats, all_stats, queries, dq_in=None):
    last = dq_in is not None
    dq_shape = (GROUP, HD, QT)
    args = [kv, all_stats, *probs, *stats, *queries]
    out_shape = [shape_of((ZS, TOK, 2 * HD), F32 if last else BF16)]
    scratch = [
        pltpu.VMEM((GROUP, QT, HD), BF16),
        pltpu.VMEM((GROUP, QT, HD), BF16),
        pltpu.VMEM((8, QT), F32),
    ]
    if last:
        args.append(dq_in)
        out_shape += [shape_of((TOK, WIDE), F32)] + [shape_of((TOK, WIDE), BF16)] * (YS - 1)
        scratch.append(pltpu.VMEM(dq_shape, F32))
    else:
        out_shape.append(shape_of(dq_shape, F32))
    return pl.pallas_call(
        functools.partial(grad_kernel, last, len(probs)),
        in_specs=[VMEM] * len(args),
        out_specs=[VMEM] * len(out_shape),
        out_shape=out_shape,
        scratch_shapes=scratch,
        compiler_params=params(),
        cost_estimate=cost("grads"),
        name="grads",
    )(*args)


def per_device(query, key_rows, value_rows, output, grad_out, block_order, segment):
    n = lax.axis_size("ctx")
    key_groups = [[r + 8 * z for z in range(ZS)] for r in range(ZS)]
    tile_groups = [[c + 8 * z + bits for bits in TILE] for z in range(ZS) for c in range(2)]

    def swap(x, bits):
        return lax.ppermute(x, "ctx", [(i, i ^ bits) for i in range(n)])

    def exchange(x, groups):
        return lax.all_to_all(x, "ctx", 0, 0, tiled=True, axis_index_groups=groups)

    kv_pay, q_pay = pack(
        block_order, segment.reshape(1, TOK), query, key_rows, value_rows, output, grad_out
    )
    kv_own = exchange(kv_pay, key_groups)
    q_far, q_near = swap(q_pay, TILE[2]), swap(q_pay, TILE[1])
    queries = [q_pay, q_near, q_far, swap(q_far, TILE[1])]
    kv_twin = swap(kv_own, 1)
    index = lax.axis_index("ctx").astype(jnp.int32)
    place = (index >> 1 & (YS - 1)).reshape(1)
    near, far = queries[:3], queries[3:]
    p_near, st_near = scores("near", kv_own, near)
    p_near_twin, st_near_twin = scores("near_twin", kv_twin, near)
    st_near_twin, far = lax.optimization_barrier((st_near_twin, far))
    queries = near + far
    p_far, st_far = scores("far", kv_own, far)
    prev = (st_near, st_near_twin, st_far)
    p_far_twin, st_far_twin, stats = scores("far_twin", kv_twin, far, prev, place)
    all_stats = exchange(stats, tile_groups)
    dkv_twin, dq = grads(
        kv_twin, [p_near_twin, p_far_twin], [st_near_twin, st_far_twin], all_stats, queries
    )
    dkv_back = swap(dkv_twin, 1)
    dkv_own, dq_own, *dq_send = grads(
        kv_own, [p_near, p_far], [st_near, st_far], all_stats, queries, dq
    )
    dkv = (dkv_own + dkv_back.astype(F32)).astype(BF16)
    dkv_all = exchange(dkv, key_groups)
    dq_parts = [swap(part, bits) for part, bits in zip(dq_send[::-1], TILE[:0:-1])]
    grad_query = dq_own + sum(part.astype(F32) for part in dq_parts)
    grad_kv = jnp.sum(dkv_all.astype(F32), axis=0).astype(BF16)
    return grad_query.astype(BF16), grad_kv[:, 0:HD], grad_kv[:, HD : 2 * HD]


def solution(mesh):
    both = P("ctx", "kvh")
    return jax.shard_map(
        per_device,
        mesh=mesh,
        in_specs=(both, both, both, both, both, P("ctx"), P("ctx")),
        out_specs=(both, both, both),
        check_vma=False,
    )
```
